32 devices in a mesh: rep: 4 (over x, core), shard: 4 (over z), tp: 2 (over y).
Axes of the slice: x: 2, y: 2, z: 4, core: 2. Of those that a mesh axis runs over, the one named last changes fastest.
Arguments:
- expert_change: float32 [4, 4, 768, 3072], P('rep', None, 'shard', 'tp'), may hold values from -6 to 6
- table_change: float32 [4, 768, 16384], P('rep', 'shard', 'tp'), may hold values from -6 to 6
- expert_master: float32 [4, 3072, 768], P(None, 'shard'), may hold values from -6 to 6
- expert_moment: float32 [4, 3072, 768], P(None, 'shard'), may hold values from -6 to 6
- table_master: float32 [16384, 768], P('shard'), may hold values from -6 to 6
- table_moment: float32 [16384, 768], P('shard'), may hold values from -6 to 6
Outputs:
- expert_weights: float32 [4, 3072, 768], P(None, 'shard')
- expert_velocity: float32 [4, 3072, 768], P(None, 'shard')
- expert_copies: bfloat16 [4, 768, 3072], P(None, 'shard', 'tp')
- table_weights: float32 [16384, 768], P('shard')
- table_velocity: float32 [16384, 768], P('shard')
- table_copies: bfloat16 [768, 16384], P('shard', 'tp')
The draws below stay inside these ranges and needn't reach their ends.
All inputs are finite; a program needn't handle non-finite values.
Results may differ from the reference program's by a relative error of at most 0.001.
Values may be sent and summed in bfloat16 or wider, within the bound.
No kernel may reach another device: no remote copies, remote signals or barrier semaphores. Data moves between devices by JAX's collectives and lax.ppermute only.
A program may use at most 256 MiB of HBM per device.

```python
import jax
import jax.numpy as jnp

D = 768
FF = 3072
VOCAB = 16384
MATS = 4
N_REP = 4


def level_of(key, dims, shards, low, largest):
    factor_of, own = 1.0, jax.random.fold_in(key, 6)
    for position, parts in shards:
        heights = jnp.exp(jax.random.uniform(jax.random.fold_in(own, position), (parts,), jnp.float32, low / len(shards), largest / len(shards)))
        factor_of = factor_of * jnp.repeat(heights, dims[position] // parts).reshape([-1 if axis == position else 1 for axis in range(len(dims))])
    return factor_of


def gaussian(rng, shape, spread, most, pieces=(), dtype=jnp.bfloat16):
    array = spread * jax.random.normal(rng, shape, jnp.float32)
    if pieces:
        array = array * level_of(rng, shape, pieces, -0.22, 0.18)
    return jnp.clip(array, -most, most).astype(dtype)


def setup_inputs(seed: int = 0) -> dict:
    splits = jax.random.split(jax.random.key(seed), 7)
    expert_change = gaussian(splits[0], (N_REP, MATS, D, FF), 1.0, 6.0, ((0, 4), (2, 4), (3, 2)), jnp.float32)
    table_change = gaussian(splits[1], (N_REP, D, VOCAB), 1.0, 6.0, ((0, 4), (1, 4), (2, 2)), jnp.float32)
    expert_master = gaussian(splits[2], (MATS, FF, D), 1.0, 6.0, ((1, 4),), jnp.float32)
    expert_moment = gaussian(splits[3], (MATS, FF, D), 1.0, 6.0, ((1, 4),), jnp.float32)
    table_master = gaussian(splits[4], (VOCAB, D), 1.0, 6.0, ((0, 4),), jnp.float32)
    table_moment = gaussian(splits[5], (VOCAB, D), 1.0, 6.0, ((0, 4),), jnp.float32)
    return dict(expert_change=expert_change, table_change=table_change, expert_master=expert_master, expert_moment=expert_moment, table_master=table_master, table_moment=table_moment)


momentum_coef = 0.9
outer_rate = 0.7


def reference(expert_change, table_change, expert_master, expert_moment, table_master, table_moment):
    expert_mean = jnp.transpose(jnp.sum(expert_change, axis=0), (0, 2, 1)) / N_REP
    table_mean = jnp.transpose(jnp.sum(table_change, axis=0)) / N_REP
    expert_velocity = momentum_coef * expert_moment + expert_mean
    expert_weights = expert_master - outer_rate * (expert_mean + momentum_coef * expert_velocity)
    expert_copies = jnp.transpose(expert_weights, (0, 2, 1)).astype(jnp.bfloat16)
    table_velocity = momentum_coef * table_moment + table_mean
    table_weights = table_master - outer_rate * (table_mean + momentum_coef * table_velocity)
    table_copies = jnp.transpose(table_weights).astype(jnp.bfloat16)
    return (expert_weights, expert_velocity, expert_copies, table_weights, table_velocity, table_copies)
```

```python
import jax
import jax.numpy as jnp
from jax import lax
from jax.sharding import PartitionSpec as P

momentum_coef = 0.9
outer_rate = 0.7
axes = ("rep", "shard", "tp")
scale = 2048.0


def pairs(mesh_sizes, move):
    groups, shards, tensor = mesh_sizes
    result = []
    for r in range(groups):
        for z in range(shards):
            for y in range(tensor):
                r2, z2, y2 = move(r, z, y)
                result.append(((r * shards + z) * tensor + y, (r2 * shards + z2) * tensor + y2))
    return result


def local(expert_change, table_change, expert_master, expert_moment, table_master, table_moment):
    groups, shards, tensor = sizes = tuple(lax.axis_size(a) for a in axes)
    r, z, y = (lax.axis_index(a) for a in axes)
    core, x = r % 2, r // 2
    half_shards = shards // tensor
    mine = (z % half_shards) * tensor + y

    def send(value, move):
        return lax.ppermute(value, axes, pairs(sizes, move))

    def over_core(value):
        return send(value, lambda r, z, y: (r ^ 1, z, y))

    def over_x(value):
        return send(value, lambda r, z, y: (r ^ 2, z, y))

    def over_y(value):
        return send(value, lambda r, z, y: (r, z, y ^ 1))

    def scatter_to(k):
        def move(r, z, y):
            p = (z + k) % shards
            return r, y * half_shards + p // tensor, p % tensor

        return move

    def gather_from(k):
        def move(r, z, y):
            p = (z % half_shards) * tensor + y
            return r, (p - k) % shards, z // half_shards

        return move

    def piece(value, p, width):
        return lax.dynamic_slice_in_dim(value, p * width, width, value.ndim - 1)

    def reduce_part(own, other):
        half = own + over_core(other)
        sent = lax.dynamic_index_in_dim(half, 1 - x, 0, False)
        kept = lax.dynamic_index_in_dim(half, x, 0, False)
        received = over_x((sent * scale).astype(jnp.float16))
        return (kept * scale + received.astype(jnp.float32)).astype(jnp.float16)

    def scatter_part(total):
        rows, width = total.shape[0], total.shape[1] // shards
        result = jnp.zeros((shards, rows, width), total.dtype)
        for k in range(shards):
            got = send(piece(total, (z + k) % shards, width), scatter_to(k))
            result = lax.dynamic_update_index_in_dim(result, got, (mine - k) % shards, 0)
        return result

    def copies_part(low):
        rows, width = low.shape[1:]
        result = jnp.zeros((rows, shards * width), low.dtype)
        for k in range(shards):
            got = send(lax.dynamic_index_in_dim(low, (mine - k) % shards, 0, False), gather_from(k))
            result = lax.dynamic_update_slice_in_dim(result, got, ((z + k) % shards) * width, 1)
        return result

    def gather_part(own):
        result = jnp.zeros((2, 2, 2) + own.shape, own.dtype)
        near = over_x(own)
        pieces = {(0, 0): own, (1, 0): near, (0, 1): over_y(own), (1, 1): over_y(near)}
        for (dx, dy), value in pieces.items():
            for dc, part in ((0, value), (1, over_core(value))):
                place = (core ^ dc, x ^ dx, y ^ dy, 0, 0)
                result = lax.dynamic_update_slice(result, part[None, None, None], place)
        return result

    def quarter(a, width):
        return lax.dynamic_slice(a, (core, x, y, 0, 0), (1, 1, 1) + a.shape[3:])[0, 0, 0]

    def step(received, master, moment):
        rows, width = received.shape[1:]
        model = shards * rows
        summed = jnp.transpose(received, (2, 0, 1)).reshape(width, model)
        gathered = gather_part(summed)
        base = quarter(master, width) - outer_rate * momentum_coef * momentum_coef * quarter(moment, width)
        base = jnp.transpose(base).reshape(shards, rows, width)
        low = base - (outer_rate * (1 + momentum_coef) / (groups * scale)) * received.astype(jnp.float32)
        copies = copies_part(low.astype(jnp.bfloat16))
        mean = gathered.astype(jnp.float32) * (1 / (groups * scale))
        velocity = momentum_coef * moment + mean
        weights = master - outer_rate * (mean + momentum_coef * velocity)
        return weights, velocity, copies

    mats, rows, expert_columns = expert_change.shape[1:]
    change = expert_change[0].reshape(2, 2, rows, expert_columns)
    expert_total = reduce_part(
        lax.dynamic_index_in_dim(change, core, 0, False),
        lax.dynamic_index_in_dim(change, 1 - core, 0, False),
    )
    table = table_change[0]
    table_columns = table.shape[1]
    block = table_columns // half_shards
    width = block // 8

    def of_core(c):
        both = []
        for dx in range(2):
            both.append(
                jnp.concatenate(
                    [
                        lax.dynamic_slice_in_dim(table, a * block + c * 4 * width + dx * 2 * width, 2 * width, 1)
                        for a in range(half_shards)
                    ],
                    1,
                )
            )
        return jnp.stack(both)

    table_total = reduce_part(of_core(core), of_core(1 - core))
    expert_received = scatter_part(expert_total)
    table_received = scatter_part(table_total)

    model = expert_master.shape[-1]
    expert_shape = (2, 2, tensor, expert_master.shape[1] // tensor, model)
    table_shape = (2, 2, tensor, width, model)
    expert_weights, expert_velocity, expert_low = step(
        expert_received, expert_master.reshape(expert_shape), expert_moment.reshape(expert_shape)
    )
    table_weights, table_velocity, table_low = step(
        table_received, table_master.reshape(table_shape), table_moment.reshape(table_shape)
    )

    near = over_x(expert_low)
    result = jnp.zeros((2, 2) + expert_low.shape, expert_low.dtype)
    for dx, value in ((0, expert_low), (1, near)):
        for dc, part in ((0, value), (1, over_core(value))):
            result = lax.dynamic_update_slice(result, part[None, None], (core ^ dc, x ^ dx, 0, 0))
    expert_copies = result.reshape(mats, rows, expert_columns)
    near = over_x(table_low)
    table_copies = jnp.zeros((rows, table_columns), table_low.dtype)
    for dx, value in ((0, table_low), (1, near)):
        for dc, part in ((0, value), (1, over_core(value))):
            for a in range(half_shards):
                table_copies = lax.dynamic_update_slice(
                    table_copies,
                    part[:, a * 2 * width : (a + 1) * 2 * width],
                    (0, a * block + (core ^ dc) * 4 * width + (x ^ dx) * 2 * width),
                )
    return (
        expert_weights.reshape(expert_master.shape),
        expert_velocity.reshape(expert_master.shape),
        expert_copies,
        table_weights.reshape(table_master.shape),
        table_velocity.reshape(table_master.shape),
        table_copies,
    )


def solution(mesh):
    in_specs = (
        P("rep", None, "shard", "tp"),
        P("rep", "shard", "tp"),
        P(None, "shard", None),
        P(None, "shard", None),
        P("shard", None),
        P("shard", None),
    )
    out_specs = (
        P(None, "shard", None),
        P(None, "shard", None),
        P(None, "shard", "tp"),
        P("shard", None),
        P("shard", None),
        P("shard", "tp"),
    )
    return jax.shard_map(local, mesh=mesh, in_specs=in_specs, out_specs=out_specs, check_vma=False)
```

```python
import jax
import jax.numpy as jnp
from jax import lax
from jax.experimental import pallas as pl
from jax.experimental.pallas import tpu as pltpu
from jax.sharding import PartitionSpec as P

momentum_coef = 0.9
outer_rate = 0.7
axes = ("rep", "shard", "tp")
scale = 2048.0
vmem = 52 * 2**20


def pairs(mesh_sizes, move):
    groups, shards, tensor = mesh_sizes
    result = []
    for r in range(groups):
        for z in range(shards):
            for y in range(tensor):
                r2, z2, y2 = move(r, z, y)
                result.append(((r * shards + z) * tensor + y, (r2 * shards + z2) * tensor + y2))
    return result


class Table:
    def __init__(self, rows, width, half_shards, tensor):
        self.shape = (rows, half_shards * 4 * tensor * width)
        self.tensor, self.width = tensor, width

    def block(self, c, x, a, h):
        rows = self.shape[0]
        if h is None:
            return (rows, self.tensor * self.width), (0, (a * 2 + c) * 2 + x)
        return (rows, self.width), (0, ((a * 2 + c) * 2 + x) * self.tensor + h)


class Expert:
    def __init__(self, rows, width, half_shards, tensor):
        self.shape = (2, 2, rows, half_shards * tensor * width)
        self.tensor, self.width = tensor, width

    def block(self, c, x, a, h):
        rows = self.shape[2]
        if h is None:
            return (1, 1, rows, self.tensor * self.width), (c, x, 0, a)
        return (1, 1, rows, self.width), (c, x, 0, a * self.tensor + h)


def aligned(rows, width):
    return rows % 16 == 0 and width % 128 == 0


def cut(layout, value, c, x, a):
    shape, at = layout.block(c, x, a, None)
    start = [i * n for i, n in zip(at, shape)]
    return lax.dynamic_slice(value, start, shape).reshape(layout.shape[-2], layout.tensor * layout.width)


def call(kernel, name, grid, scalars, inputs, outputs, aliases, cost):
    in_specs = [
        pl.BlockSpec(memory_space=pl.ANY) if block is None else pl.BlockSpec(block, at)
        for _, block, at in inputs
    ]
    grid_spec = pltpu.PrefetchScalarGridSpec(
        num_scalar_prefetch=1,
        grid=grid,
        in_specs=in_specs,
        out_specs=[pl.BlockSpec(block, at) for _, _, block, at in outputs],
    )
    return pl.pallas_call(
        kernel,
        grid_spec=grid_spec,
        out_shape=[jax.ShapeDtypeStruct(shape, dtype) for shape, dtype, _, _ in outputs],
        input_output_aliases=aliases,
        compiler_params=pltpu.CompilerParams(vmem_limit_bytes=vmem),
        cost_estimate=pl.CostEstimate(flops=20000000000, bytes_accessed=1000000, transcendentals=0),
        name=name,
    )(scalars, *[array for array, _, _ in inputs])


def pick(layout, value, here, half_shards):
    rows, wide = layout.shape[-2], layout.tensor * layout.width
    if not aligned(rows, layout.width):
        parts = [cut(layout, value, here[0], x, a) for x in range(2) for a in range(half_shards)]
        return jnp.stack(parts).reshape(2, half_shards, rows, wide)

    def kernel(here, value_ref, out_ref):
        out_ref[...] = value_ref[...].reshape(out_ref.shape)

    block = layout.block(0, 0, 0, None)[0]
    return call(
        kernel,
        "pick",
        (2, half_shards),
        here,
        [(value, block, lambda x, a, here: layout.block(here[0], x, a, None)[1])],
        [((2, half_shards, rows, wide), value.dtype, (1, 1, rows, wide), lambda x, a, here: (x, a, 0, 0))],
        {},
        2 * half_shards * rows * wide * 16,
    )[0]


def add_split(layout, value, received, here, half_shards):
    rows, tensor, width = layout.shape[-2], layout.tensor, layout.width
    if not aligned(rows, width):
        halves = []
        for x in (1 - here[1], here[1]):
            own = jnp.stack([cut(layout, value, here[0], x, a) for a in range(half_shards)])
            halves.append(own + lax.dynamic_index_in_dim(received, x, 0, False))
        return halves

    def kernel(here, own_sent, own_kept, got_sent, got_kept, sent_ref, kept_ref):
        shape = sent_ref.shape
        sent_ref[...] = own_sent[...].reshape(shape) + got_sent[...].reshape(shape)
        kept_ref[...] = own_kept[...].reshape(shape) + got_kept[...].reshape(shape)

    block = layout.block(0, 0, 0, 0)[0]
    got_block = (1, 1, rows, width)
    out_block = (1, rows, width)
    out_at = lambda a, h, here: (a, 0, h)
    out = ((half_shards, rows, tensor * width), jnp.float32, out_block, out_at)
    return call(
        kernel,
        "add_split",
        (half_shards, tensor),
        here,
        [
            (value, block, lambda a, h, here: layout.block(here[0], 1 - here[1], a, h)[1]),
            (value, block, lambda a, h, here: layout.block(here[0], here[1], a, h)[1]),
            (received, got_block, lambda a, h, here: (1 - here[1], a, 0, h)),
            (received, got_block, lambda a, h, here: (here[1], a, 0, h)),
        ],
        [out, out],
        {},
        half_shards * rows * tensor * width * 24,
    )


def transposed_base(master, moment, here):
    width, model = master.shape[-2:]
    step = 128
    if not aligned(model, width):
        start, shape = (here[0], here[1], here[2], 0, 0), (1, 1, 1, width, model)
        base = lax.dynamic_slice(master, start, shape) - (
            outer_rate * momentum_coef * momentum_coef
        ) * lax.dynamic_slice(moment, start, shape)
        return base[0, 0, 0].T

    def kernel(here, master_ref, moment_ref, out_ref):
        shape = (step, model)
        base = master_ref[...].reshape(shape) - (
            outer_rate * momentum_coef * momentum_coef
        ) * moment_ref[...].reshape(shape)
        out_ref[...] = base.T

    at = lambda i, here: (here[0], here[1], here[2], i, 0)
    block = (1, 1, 1, step, model)
    return call(
        kernel,
        "transposed_base",
        (width // step,),
        here,
        [(master, block, at), (moment, block, at)],
        [((model, width), jnp.float32, (model, step), lambda i, here: (0, i))],
        {},
        model * width * 12,
    )[0]


def update(parts, master, moment, here, before):
    width, model = master.shape[-2:]
    if not aligned(model, width):
        weights, velocity = before or (jnp.zeros_like(master), jnp.zeros_like(moment))
        for d in range(2):
            start, shape = (here[0], here[1] ^ d, here[2], 0, 0), (1, 1, 1, width, model)
            mean = parts[d].reshape(shape) * (1 / (4 * scale))
            new = momentum_coef * lax.dynamic_slice(moment, start, shape) + mean
            velocity = lax.dynamic_update_slice(velocity, new, start)
            new = lax.dynamic_slice(master, start, shape) - outer_rate * (mean + momentum_coef * new)
            weights = lax.dynamic_update_slice(weights, new, start)
        return weights, velocity

    def kernel(here, own_ref, near_ref, master_ref, moment_ref, *refs):
        weights_ref, velocity_ref = refs[-2:]

        def compute(summed_ref):
            mean = summed_ref[...].reshape(weights_ref.shape) * (1 / (4 * scale))
            velocity = momentum_coef * moment_ref[...] + mean
            velocity_ref[...] = velocity
            weights_ref[...] = master_ref[...] - outer_rate * (mean + momentum_coef * velocity)

        @pl.when(pl.program_id(0) == 0)
        def _():
            compute(own_ref)

        @pl.when(pl.program_id(0) == 1)
        def _():
            compute(near_ref)

    at = lambda d, here: (here[0], here[1] ^ d, here[2], 0, 0)
    block = (1, 1, 1, width, model)
    out = (master.shape, jnp.float32, block, at)
    inputs = [(part, (width, model), lambda d, here: (0, 0)) for part in parts]
    inputs += [(master, block, at), (moment, block, at)]
    aliases = {}
    if before is not None:
        inputs += [(value, None, None) for value in before]
        aliases = {5: 0, 6: 1}
    return call(kernel, "update", (2,), here, inputs, [out, out], aliases, 2 * width * model * 20)


def place(layout, parts, here, before, half_shards):
    rows, width, tensor = layout.shape[-2], layout.width, layout.tensor
    if not aligned(rows, width):
        result = jnp.zeros(layout.shape, jnp.bfloat16) if before is None else before
        for j, part in enumerate(parts):
            for a in range(half_shards):
                shape, at = layout.block(here[0], here[1] ^ (j // 2), a, here[2] ^ (j % 2))
                start = [i * n for i, n in zip(at, shape)]
                result = lax.dynamic_update_slice(result, part[a].reshape(shape), start)
        return result

    def kernel(here, *refs):
        out_ref = refs[-1]
        lead = (0,) * (len(out_ref.shape) - 2)
        for x in range(2):
            for y in range(tensor):

                @pl.when((pl.program_id(0) == x) & (here[2] == y))
                def _():
                    for t in range(tensor):
                        out_ref[lead + (slice(None), slice((y ^ t) * width, ((y ^ t) + 1) * width))] = refs[2 * x + t][0]

    def part_at(x):
        if x == 0:
            return lambda d, a, here: (jnp.where(d == 0, a, half_shards - 1), 0, 0)
        return lambda d, a, here: (jnp.where(d == 1, a, 0), 0, 0)

    block = layout.block(0, 0, 0, None)[0]
    out_at = lambda d, a, here: layout.block(here[0], here[1] ^ d, a, None)[1]
    inputs = [(part, (1, rows, width), part_at(j // 2)) for j, part in enumerate(parts)]
    aliases = {}
    if before is not None:
        inputs.append((before, None, None))
        aliases = {5: 0}
    return call(
        kernel,
        "place",
        (2, half_shards),
        here,
        inputs,
        [(layout.shape, jnp.bfloat16, block, out_at)],
        aliases,
        4 * half_shards * rows * width * 4,
    )[0]


def local(expert_change, table_change, expert_master, expert_moment, table_master, table_moment):
    groups, shards, tensor = sizes = tuple(lax.axis_size(a) for a in axes)
    r, z, y = (lax.axis_index(a) for a in axes)
    core, x = r % 2, r // 2
    half_shards = shards // tensor
    here = jnp.stack([core, x, y]).astype(jnp.int32)
    other = jnp.stack([1 - core, x, y]).astype(jnp.int32)
    here_far = jnp.stack([core, x, 1 - y]).astype(jnp.int32)
    other_far = jnp.stack([1 - core, x, 1 - y]).astype(jnp.int32)

    def send(name, value, move):
        with jax.named_scope(name):
            return lax.ppermute(value, axes, pairs(sizes, move))

    def over_core(name, value):
        return send(name + "_core", value, lambda r, z, y: (r ^ 1, z, y))

    def over_x(name, value):
        return send(name + "_x", value, lambda r, z, y: (r ^ 2, z, y))

    def over_y(name, value):
        return send(name + "_y", value, lambda r, z, y: (r, z, y ^ 1))

    def over_z(name, value):
        with jax.named_scope(name + "_z"):
            return lax.all_to_all(value, "shard", split_axis=0, concat_axis=0, tiled=True)

    def index(value, i):
        return lax.dynamic_index_in_dim(value, i, 0, False)

    last = []

    def after(*values):
        if not last:
            return values if len(values) > 1 else values[0]
        values = lax.optimization_barrier((*values, last[0]))[:-1]
        return values if len(values) > 1 else values[0]

    def mark(value):
        last[:] = [value]
        return value

    def unmix(got):
        k = 1
        while k < shards:
            swap = (z & k) != 0
            got = [jnp.where(swap, got[i ^ k], got[i]) for i in range(shards)]
            k *= 2
        return got

    model = expert_master.shape[-1]
    mats, rows, expert_columns = expert_change.shape[1:]

    class Part:
        def __init__(self, name, layout, change, master, moment):
            self.name, self.layout, self.change = name, layout, change
            shape = (2, 2, tensor, layout.width, model)
            self.master, self.moment = master.reshape(shape), moment.reshape(shape)
            self.result = None

        def start(self):
            picked = mark(pick(self.layout, after(self.change), other, half_shards))
            self.got = over_core(self.name, picked)

        def sum_core(self):
            change, got = after(self.change, self.got)
            sent, self.kept = add_split(self.layout, change, got, here, half_shards)
            self.received = over_x(self.name, mark((sent * scale).astype(jnp.float16)))

        def bases(self):
            master, moment = after(self.master, self.moment)
            self.base = mark(transposed_base(master, moment, here))

        def sum_x(self):
            kept, received = after(self.kept, self.received)
            width = self.layout.width
            total = (kept * scale + received.astype(jnp.float32)).astype(jnp.float16)
            self.near = lax.dynamic_slice_in_dim(total, y * width, width, 2)
            self.far = over_y(self.name, mark(lax.dynamic_slice_in_dim(total, (1 - y) * width, width, 2)))

        def scatter(self):
            near, far = after(self.near, self.far)

            def of_shard(s):
                a = s % half_shards
                return jnp.where(s // half_shards == y, index(near, a), index(far, a))

            sent = [of_shard(z ^ k) for k in range(shards)]
            mark(sent[-1])
            self.sums = [sent[0]] + [
                send(f"{self.name}_z{k}", sent[k], lambda r, z, y: (r, z ^ k, y)) for k in range(1, shards)
            ]

        def low_part(self):
            received = after(self.received)
            base = self.base.reshape(received.shape)
            low = base - (outer_rate * (1 + momentum_coef) / (groups * scale)) * received.astype(jnp.float32)
            self.low = mark(low.astype(jnp.bfloat16))

        def copies_z(self):
            self.low = over_z(self.name + "_back", mark(after(self.low)))

        def gather(self):
            self.received = received = jnp.stack(unmix(after(*self.sums)))
            own = mark(jnp.transpose(received, (2, 0, 1)).reshape(received.shape[2], model))
            self.near = over_x(self.name + "_gather", own)
            self.far = over_y(self.name + "_gather", own)
            self.own = own

        def gather_x(self):
            near = after(self.near)
            self.far2 = over_y(self.name + "_gather2", near)
            own, near = self.own.astype(jnp.float32), near.astype(jnp.float32)
            mark(near)
            self.pair = own, near
            self.pair_core = over_core(self.name + "_gather", own), over_core(self.name + "_gather", near)

        def gather_y(self):
            far, far2 = after(self.far, self.far2)
            far, far2 = far.astype(jnp.float32), far2.astype(jnp.float32)
            mark(far2)
            self.far_pair = far, far2
            self.far_core = over_core(self.name + "_gather2", far), over_core(self.name + "_gather2", far2)

        def wait(self, name):
            setattr(self, name, mark(after(getattr(self, name))))

        def update(self, which):
            parts, where = {
                "pair": lambda: (self.pair, here),
                "pair_core": lambda: (self.pair_core, other),
                "far_pair": lambda: (self.far_pair, here_far),
                "far_core": lambda: (self.far_core, other_far),
            }[which]()
            parts = after(*parts)
            self.result = update(parts, self.master, self.moment, where, self.result)
            mark(self.result[0])

        def copies_y(self):
            got = after(self.low)
            near = lax.dynamic_slice_in_dim(got, y * half_shards, half_shards, 0)
            far = mark(lax.dynamic_slice_in_dim(got, (1 - y) * half_shards, half_shards, 0))
            self.low_near = near
            self.low_far = over_y(self.name + "_back", far)
            self.low_near_x = over_x(self.name + "_back", near)
            self.low_near_core = over_core(self.name + "_back", near)

        def copies_x(self):
            far = mark(after(self.low_far))
            self.low_far = far
            self.low_far_x = over_x(self.name + "_back2", far)
            self.low_far_core = over_core(self.name + "_back2", far)

        def copies_core(self):
            near_x, far_x = after(self.low_near_x, self.low_far_x)
            mark(far_x)
            self.parts = [self.low_near, self.low_far, near_x, far_x]
            self.parts_core = [
                self.low_near_core,
                self.low_far_core,
                over_core(self.name + "_back", near_x),
                over_core(self.name + "_back2", far_x),
            ]

        def place(self):
            parts = after(*self.parts)
            self.copies = mark(place(self.layout, parts, here, None, half_shards))

        def place_core(self):
            parts = after(*self.parts_core)
            self.copies = mark(place(self.layout, parts, other, self.copies, half_shards))

    t = Part(
        "table",
        Table(rows, table_change.shape[2] // (4 * shards), half_shards, tensor),
        table_change[0],
        table_master,
        table_moment,
    )
    expert_layout = Expert(rows, expert_columns // shards, half_shards, tensor)
    e = Part(
        "expert", expert_layout, expert_change[0].reshape(expert_layout.shape), expert_master, expert_moment
    )
    e.start()
    t.start()
    e.sum_core()
    t.sum_core()
    e.bases()
    t.bases()
    e.sum_x()
    e.scatter()
    t.sum_x()
    e.gather()
    t.scatter()
    e.low_part()
    e.wait("near")
    e.wait("far")
    e.gather_x()
    e.update("pair")
    t.gather()
    e.copies_z()
    e.update("pair_core")
    e.wait("far2")
    e.gather_y()
    t.low_part()
    e.update("far_pair")
    e.copies_y()
    t.copies_z()
    t.wait("near")
    t.wait("far")
    t.gather_x()
    e.update("far_core")
    e.wait("low_near_x")
    e.copies_x()
    t.update("pair")
    t.update("pair_core")
    t.copies_y()
    t.wait("far2")
    t.gather_y()
    e.copies_core()
    e.place()
    e.place_core()
    t.wait("low_near_x")
    t.copies_x()
    t.update("far_pair")
    t.copies_core()
    t.update("far_core")
    t.place()
    t.place_core()
    return (
        e.result[0].reshape(expert_master.shape),
        e.result[1].reshape(expert_master.shape),
        e.copies.reshape(mats, rows, expert_columns),
        t.result[0].reshape(table_master.shape),
        t.result[1].reshape(table_master.shape),
        t.copies,
    )


def solution(mesh):
    in_specs = (
        P("rep", None, "shard", "tp"),
        P("rep", "shard", "tp"),
        P(None, "shard", None),
        P(None, "shard", None),
        P("shard", None),
        P("shard", None),
    )
    out_specs = (
        P(None, "shard", None),
        P(None, "shard", None),
        P(None, "shard", "tp"),
        P("shard", None),
        P("shard", None),
        P("shard", "tp"),
    )
    return jax.shard_map(local, mesh=mesh, in_specs=in_specs, out_specs=out_specs, check_vma=False)
```

```python
import jax
import jax.numpy as jnp
from jax import lax
from jax.experimental import pallas as pl
from jax.experimental.layout import Layout, with_layout_constraint
from jax.experimental.pallas import tpu as pltpu
from jax.sharding import PartitionSpec as P

momentum_coef = 0.9
outer_rate = 0.7
axes = ("rep", "shard", "tp")
scale = 2048.0
vmem = 52 * 2**20


def pairs(mesh_sizes, move):
    groups, shards, tensor = mesh_sizes
    result = []
    for r in range(groups):
        for z in range(shards):
            for y in range(tensor):
                r2, z2, y2 = move(r, z, y)
                result.append(((r * shards + z) * tensor + y, (r2 * shards + z2) * tensor + y2))
    return result


class Table:
    table = True

    def __init__(self, rows, width, half_shards, tensor):
        self.shape = (rows, half_shards * 4 * tensor * width)
        self.tensor, self.width = tensor, width

    def block(self, c, x, a, h):
        rows = self.shape[0]
        if h is None:
            return (rows, self.tensor * self.width), (0, (a * 2 + c) * 2 + x)
        return (rows, self.width), (0, ((a * 2 + c) * 2 + x) * self.tensor + h)


class Expert:
    table = False

    def __init__(self, rows, width, half_shards, tensor):
        self.shape = (2, 2, rows, half_shards * tensor * width)
        self.tensor, self.width = tensor, width

    def block(self, c, x, a, h):
        rows = self.shape[2]
        if h is None:
            return (1, 1, rows, self.tensor * self.width), (c, x, 0, a)
        return (1, 1, rows, self.width), (c, x, 0, a * self.tensor + h)


def aligned(rows, width):
    return rows % 16 == 0 and width % 128 == 0


def cut(layout, value, c, x, a):
    shape, at = layout.block(c, x, a, None)
    start = [i * n for i, n in zip(at, shape)]
    return lax.dynamic_slice(value, start, shape).reshape(layout.shape[-2], layout.tensor * layout.width)


def call(kernel, name, grid, scalars, inputs, outputs, aliases):
    in_specs = [
        pl.BlockSpec(memory_space=pl.ANY) if block is None else pl.BlockSpec(block, at)
        for _, block, at in inputs
    ]
    grid_spec = pltpu.PrefetchScalarGridSpec(
        num_scalar_prefetch=1,
        grid=grid,
        in_specs=in_specs,
        out_specs=[pl.BlockSpec(block, at) for _, _, block, at in outputs],
    )
    return pl.pallas_call(
        kernel,
        grid_spec=grid_spec,
        out_shape=[jax.ShapeDtypeStruct(shape, dtype) for shape, dtype, _, _ in outputs],
        input_output_aliases=aliases,
        compiler_params=pltpu.CompilerParams(vmem_limit_bytes=vmem),
        cost_estimate=pl.CostEstimate(flops=20000000000, bytes_accessed=1000000, transcendentals=0),
        name=name,
    )(scalars, *[array for array, _, _ in inputs])


def pick_table(layout, value, here, half_shards):
    rows, wide = layout.shape[-2], 2 * layout.tensor * layout.width
    if not aligned(rows, layout.width):
        parts = [cut(layout, value, here[0], x, a) for a in range(half_shards) for x in range(2)]
        parts = [jnp.concatenate(parts[2 * a : 2 * a + 2], 1) for a in range(half_shards)]
        return jnp.stack(parts)

    def kernel(here, value_ref, out_ref):
        out_ref[0] = value_ref[...]

    return call(
        kernel,
        "pick",
        (half_shards,),
        here,
        [(value, (rows, wide), lambda a, here: (0, a * 2 + here[0]))],
        [((half_shards, rows, wide), value.dtype, (1, rows, wide), lambda a, here: (a, 0, 0))],
        {},
    )[0]


def add_split(layout, value, received, here, half_shards):
    rows, tensor, width = layout.shape[-2], layout.tensor, layout.width
    wide = tensor * width

    def got(x, a):
        return (a, 0, x) if layout.table else (x, 0, a)

    if not aligned(rows, width):
        halves = []
        for x in (1 - here[1], here[1]):
            parts = []
            for a in range(half_shards):
                first, _, last = got(x, a)
                part = lax.dynamic_slice(received, (first, 0, last * wide), (1, rows, wide))[0]
                parts.append(part + cut(layout, value, here[0], x, a))
            for y in (1 - here[2], here[2]):
                halves.append(lax.dynamic_slice_in_dim(jnp.stack(parts), y * width, width, 2))
        return halves

    def kernel(here, own_sent, own_kept, got_sent, got_kept, *out_refs):
        for y in range(tensor):

            @pl.when(here[2] == y)
            def _():
                for j, (own, got) in enumerate(((own_sent, got_sent), (own_kept, got_kept))):
                    lead = (0,) * (len(own.shape) - 2) + (slice(None),)
                    for h in range(2):
                        start = (y ^ h ^ 1) * width
                        columns = slice(start, start + width)
                        out_refs[2 * j + h][0] = own[lead + (columns,)] + got[0, :, columns]

    block = layout.block(0, 0, 0, None)[0]
    out = ((half_shards, rows, width), jnp.float32, (1, rows, width), lambda a, here: (a, 0, 0))
    return call(
        kernel,
        "add_split",
        (half_shards,),
        here,
        [
            (value, block, lambda a, here: layout.block(here[0], 1 - here[1], a, None)[1]),
            (value, block, lambda a, here: layout.block(here[0], here[1], a, None)[1]),
            (received, (1, rows, wide), lambda a, here: got(1 - here[1], a)),
            (received, (1, rows, wide), lambda a, here: got(here[1], a)),
        ],
        [out] * 4,
        {},
    )


def transposed_base(master, moment, here):
    width, model = master.shape[-2:]
    step = 256 if width % 256 == 0 else width
    if not aligned(model, width):
        start, shape = (here[0], here[1], here[2], 0, 0), (1, 1, 1, width, model)
        base = lax.dynamic_slice(master, start, shape) - (
            outer_rate * momentum_coef * momentum_coef
        ) * lax.dynamic_slice(moment, start, shape)
        return base[0, 0, 0].T

    def kernel(here, master_ref, moment_ref, out_ref):
        shape = (step, model)
        base = master_ref[...].reshape(shape) - (
            outer_rate * momentum_coef * momentum_coef
        ) * moment_ref[...].reshape(shape)
        out_ref[...] = base.T

    at = lambda i, here: (here[0], here[1], here[2], i, 0)
    block = (1, 1, 1, step, model)
    return call(
        kernel,
        "transposed_base",
        (width // step,),
        here,
        [(master, block, at), (moment, block, at)],
        [((model, width), jnp.float32, (model, step), lambda i, here: (0, i))],
        {},
    )[0]


def update(stacks, master, moment, here, before):
    width, model = master.shape[-2:]
    if not aligned(model, width):
        weights, velocity = before or (jnp.zeros_like(master), jnp.zeros_like(moment))
        for d in range(2 * len(stacks)):
            start = (here[0] ^ (d // 2), here[1] ^ (d % 2), here[2], 0, 0)
            shape = (1, 1, 1, width, model)
            mean = stacks[d // 2][d % 2].reshape(shape) * (1 / (4 * scale))
            new = momentum_coef * lax.dynamic_slice(moment, start, shape) + mean
            velocity = lax.dynamic_update_slice(velocity, new, start)
            new = lax.dynamic_slice(master, start, shape) - outer_rate * (mean + momentum_coef * new)
            weights = lax.dynamic_update_slice(weights, new, start)
        return weights, velocity
    count = len(stacks)

    def kernel(here, *refs):
        master_ref, moment_ref = refs[count : count + 2]
        weights_ref, velocity_ref = refs[-2:]

        def compute(summed_ref):
            mean = summed_ref[...].reshape(weights_ref.shape) * (1 / (4 * scale))
            velocity = momentum_coef * moment_ref[...] + mean
            velocity_ref[...] = velocity
            weights_ref[...] = master_ref[...] - outer_rate * (mean + momentum_coef * velocity)

        if count == 1:
            compute(refs[0])
        else:
            for j in range(count):
                pl.when(pl.program_id(0) // 2 == j)(lambda: compute(refs[j]))

    def stack_at(j):
        return lambda d, here: (jnp.clip(d - 2 * j, 0, 1), 0, 0)

    at = lambda d, here: (here[0] ^ (d // 2), here[1] ^ (d % 2), here[2], 0, 0)
    block = (1, 1, 1, width, model)
    out = (master.shape, jnp.float32, block, at)
    inputs = [(stack, (1, width, model), stack_at(j)) for j, stack in enumerate(stacks)]
    inputs += [(master, block, at), (moment, block, at)]
    aliases = {}
    if before is not None:
        inputs += [(value, None, None) for value in before]
        aliases = {count + 3: 0, count + 4: 1}
    return call(kernel, "update", (2 * count,), here, inputs, [out, out], aliases)


def place(layout, parts, here, half_shards):
    rows, width, tensor = layout.shape[-2], layout.width, layout.tensor
    if not aligned(rows, width):
        result = jnp.zeros(layout.shape, jnp.bfloat16)
        for j, part in enumerate(parts):
            for a in range(half_shards):
                at = here[0] ^ (j // 4), here[1] ^ (j // 2 % 2), a, here[2] ^ (j % 2)
                shape, at = layout.block(*at)
                start = [i * n for i, n in zip(at, shape)]
                result = lax.dynamic_update_slice(result, part[a].reshape(shape), start)
        return result

    def kernel(here, *refs):
        out_ref = refs[-1]
        for j in range(8):
            for y in range(tensor):

                @pl.when(here[2] == y)
                def _():
                    h = y ^ (j % 2)
                    c, x = here[0] ^ (j // 4), here[1] ^ (j // 2 % 2)
                    if layout.table:
                        for place in range(4):

                            @pl.when(c * 2 + x == place)
                            def _():
                                start = (place * tensor + h) * width
                                out_ref[:, start : start + width] = refs[j][0]

                    else:
                        out_ref[c, x, :, h * width : (h + 1) * width] = refs[j][0]

    if layout.table:
        block, out_at = (rows, 4 * tensor * width), lambda a, here: (0, a)
    else:
        block, out_at = (2, 2, rows, tensor * width), lambda a, here: (0, 0, 0, a)
    return call(
        kernel,
        "place",
        (half_shards,),
        here,
        [(part, (1, rows, width), lambda a, here: (a, 0, 0)) for part in parts],
        [(layout.shape, jnp.bfloat16, block, out_at)],
        {},
    )[0]


def local(expert_change, table_change, expert_master, expert_moment, table_master, table_moment):
    groups, shards, tensor = sizes = tuple(lax.axis_size(a) for a in axes)
    r, z, y = (lax.axis_index(a) for a in axes)
    core, x = r % 2, r // 2
    half_shards = shards // tensor
    here = jnp.stack([core, x, y]).astype(jnp.int32)
    other = jnp.stack([1 - core, x, y]).astype(jnp.int32)
    here_far = jnp.stack([core, x, 1 - y]).astype(jnp.int32)
    other_far = jnp.stack([1 - core, x, 1 - y]).astype(jnp.int32)

    def send(name, value, move):
        with jax.named_scope(name):
            return lax.ppermute(value, axes, pairs(sizes, move))

    def over_core(name, value):
        return send(name + "_core", value, lambda r, z, y: (r ^ 1, z, y))

    def over_x(name, value):
        return send(name + "_x", value, lambda r, z, y: (r ^ 2, z, y))

    def over_y(name, value):
        return send(name + "_y", value, lambda r, z, y: (r, z, y ^ 1))

    def over_z(name, value):
        with jax.named_scope(name + "_z"):
            return lax.all_to_all(value, "shard", split_axis=0, concat_axis=0, tiled=True)

    def index(value, i):
        return lax.dynamic_index_in_dim(value, i, 0, False)

    last = []

    def after(*values):
        if not last:
            return values if len(values) > 1 else values[0]
        values = lax.optimization_barrier((*values, last[0]))[:-1]
        return values if len(values) > 1 else values[0]

    def mark(value):
        last[:] = [value]
        return value

    def unmix(got):
        k = 1
        while k < shards:
            swap = (z & k) != 0
            got = [jnp.where(swap, got[i ^ k], got[i]) for i in range(shards)]
            k *= 2
        return got

    model = expert_master.shape[-1]
    mats, rows, expert_columns = expert_change.shape[1:]

    class Part:
        def __init__(self, name, layout, change, master, moment):
            self.name, self.layout, self.change = name, layout, change
            shape = (2, 2, tensor, layout.width, model)
            self.master, self.moment = master.reshape(shape), moment.reshape(shape)
            self.result = None
            self.split = False

        def start(self):
            change = after(self.change)
            if self.layout.table:
                picked = pick_table(self.layout, change, other, half_shards)
            else:
                picked = index(change, 1 - core)
            self.got = over_core(self.name, mark(picked))

        def sum_core(self):
            change, got = after(self.change, self.got)
            sent = add_split(self.layout, change, got, here, half_shards)
            self.kept = sent[2:]
            far = mark((sent[0] * scale).astype(jnp.float16))
            self.received = [over_x(self.name + "_far", far)]
            self.sent_near = sent[1]

        def send_near(self):
            near = mark((after(self.sent_near) * scale).astype(jnp.float16))
            self.received.append(over_x(self.name + "_near", near))

        def bases(self):
            master, moment = after(self.master, self.moment)
            self.base = mark(transposed_base(master, moment, here))

        def sum_half(self, i):
            kept, received = after(self.kept[i], self.received[i])
            return mark((kept * scale + received.astype(jnp.float32)).astype(jnp.float16))

        def sum_far(self):
            self.far = over_y(self.name, self.sum_half(0))

        def sum_near(self):
            self.near = self.sum_half(1)

        def scatter(self):
            near, far = after(self.near, self.far)

            def of_shard(s):
                a = s % half_shards
                return jnp.where(s // half_shards == y, index(near, a), index(far, a))

            sent = [of_shard(z ^ k) for k in range(shards)]
            mark(sent[-1])
            self.sums = [sent[0]] + [
                send(f"{self.name}_z{k}", sent[k], lambda r, z, y: (r, z ^ k, y)) for k in range(1, shards)
            ]

        def low_part(self):
            received = after(self.received)
            base = self.base.reshape(received.shape)
            low = base - (outer_rate * (1 + momentum_coef) / (groups * scale)) * received.astype(jnp.float32)
            self.low = mark(low.astype(jnp.bfloat16))

        def copies_z(self):
            self.low = over_z(self.name + "_back", mark(after(self.low)))

        def gather(self):
            self.received = received = jnp.stack(unmix(after(*self.sums)))
            own = jnp.transpose(received, (2, 0, 1)).reshape(received.shape[2], model)
            own = mark(with_layout_constraint(own, Layout(major_to_minor=(0, 1))))
            self.near = over_x(self.name + "_gather", own)
            self.far = over_y(self.name + "_gather", own)
            self.own = own

        def gather_x(self):
            near = after(self.near)
            if self.split:
                half = self.layout.width // 2
                first, second = near[:half], self.far[half:]
                mark(first)
                second = mark(after(second))
                self.far2 = over_y(self.name + "_gather2", first)
                self.far2_x = over_x(self.name + "_gather2", second)
            else:
                self.far2 = over_y(self.name + "_gather2", near)
            self.pair = mark(jnp.stack([self.own, after(near)]).astype(jnp.float32))
            self.pair_core = over_core(self.name + "_gather", self.pair)

        def gather_y(self):
            far, *far2 = after(self.far, self.far2, *([self.far2_x] if self.split else []))
            mark(far2[-1])
            far2 = jnp.concatenate(far2)
            self.far_pair = mark(jnp.stack([far, far2]).astype(jnp.float32))
            self.far_core = over_core(self.name + "_gather2", self.far_pair)

        def wait(self, name):
            setattr(self, name, mark(after(getattr(self, name))))

        def update(self, *which):
            stacks = after(*[getattr(self, name) for name in which])
            stacks = stacks if len(which) > 1 else (stacks,)
            where = {"pair": here, "pair_core": other, "far_pair": here_far, "far_core": other_far}[which[0]]
            self.result = update(stacks, self.master, self.moment, where, self.result)
            mark(self.result[0])

        def copies_y(self):
            got = after(self.low)
            near = lax.dynamic_slice_in_dim(got, y * half_shards, half_shards, 0)
            far = mark(lax.dynamic_slice_in_dim(got, (1 - y) * half_shards, half_shards, 0))
            self.low_near = near
            self.low_far = over_y(self.name + "_back", far)
            self.low_near_x = over_x(self.name + "_back", near)
            self.low_near_core = over_core(self.name + "_back", near)

        def copies_x(self):
            far = mark(after(self.low_far))
            self.low_far = far
            self.low_far_x = over_x(self.name + "_back2", far)
            self.low_far_core = over_core(self.name + "_back2", far)

        def copies_core(self):
            near_x, far_x = after(self.low_near_x, self.low_far_x)
            mark(far_x)
            self.parts = [self.low_near, self.low_far, near_x, far_x]
            self.parts_core = [
                self.low_near_core,
                self.low_far_core,
                over_core(self.name + "_back", near_x),
                over_core(self.name + "_back2", far_x),
            ]

        def place(self):
            parts = after(*self.parts, *self.parts_core)
            self.copies = mark(place(self.layout, parts, here, half_shards))

    t = Part(
        "table",
        Table(rows, table_change.shape[2] // (4 * shards), half_shards, tensor),
        table_change[0],
        table_master,
        table_moment,
    )
    expert_layout = Expert(rows, expert_columns // shards, half_shards, tensor)
    e = Part(
        "expert", expert_layout, expert_change[0].reshape(expert_layout.shape), expert_master, expert_moment
    )
    e.start()
    t.start()
    e.sum_core()
    e.send_near()
    t.sum_core()
    e.sum_far()
    t.send_near()
    e.bases()
    e.sum_near()
    e.scatter()
    t.sum_far()
    t.bases()
    e.gather()
    t.sum_near()
    t.scatter()
    e.low_part()
    e.copies_z()
    e.wait("near")
    e.wait("far")
    e.gather_x()
    e.update("pair")
    e.wait("far2")
    e.gather_y()
    e.copies_y()
    t.gather()
    t.low_part()
    e.update("pair_core")
    e.update("far_pair")
    e.update("far_core")
    t.wait("near")
    t.wait("far")
    e.wait("low_far")
    e.wait("low_near_x")
    t.gather_x()
    e.copies_x()
    t.copies_z()
    t.update("pair")
    t.update("pair_core")
    t.wait("far2")
    e.wait("low_far_x")
    t.gather_y()
    t.copies_y()
    t.update("far_pair")
    t.wait("low_near_x")
    t.wait("low_far")
    t.copies_x()
    e.copies_core()
    t.update("far_core")
    t.copies_core()
    e.place()
    t.place()
    return (
        e.result[0].reshape(expert_master.shape),
        e.result[1].reshape(expert_master.shape),
        e.copies.reshape(mats, rows, expert_columns),
        t.result[0].reshape(table_master.shape),
        t.result[1].reshape(table_master.shape),
        t.copies,
    )


def solution(mesh):
    in_specs = (
        P("rep", None, "shard", "tp"),
        P("rep", "shard", "tp"),
        P(None, "shard", None),
        P(None, "shard", None),
        P("shard", None),
        P("shard", None),
    )
    out_specs = (
        P(None, "shard", None),
        P(None, "shard", None),
        P(None, "shard", "tp"),
        P("shard", None),
        P("shard", None),
        P("shard", "tp"),
    )
    return jax.shard_map(local, mesh=mesh, in_specs=in_specs, out_specs=out_specs, check_vma=False)
```

```python
import jax
import jax.numpy as jnp
from jax import lax
from jax.experimental import pallas as pl
from jax.experimental.layout import Layout, with_layout_constraint
from jax.experimental.pallas import tpu as pltpu
from jax.sharding import PartitionSpec as P

momentum_coef = 0.9
outer_rate = 0.7
axes = ("rep", "shard", "tp")
scale = 2048.0
vmem = 52 * 2**20


def pairs(mesh_sizes, move):
    groups, shards, tensor = mesh_sizes
    result = []
    for r in range(groups):
        for z in range(shards):
            for y in range(tensor):
                r2, z2, y2 = move(r, z, y)
                result.append(((r * shards + z) * tensor + y, (r2 * shards + z2) * tensor + y2))
    return result


class Table:
    table = True

    def __init__(self, rows, width, half_shards, tensor):
        self.shape = (rows, half_shards * 4 * tensor * width)
        self.tensor, self.width = tensor, width

    def block(self, c, x, a, h):
        rows = self.shape[0]
        if h is None:
            return (rows, self.tensor * self.width), (0, (a * 2 + c) * 2 + x)
        return (rows, self.width), (0, ((a * 2 + c) * 2 + x) * self.tensor + h)


class Expert:
    table = False

    def __init__(self, rows, width, half_shards, tensor):
        self.shape = (2, 2, rows, half_shards * tensor * width)
        self.tensor, self.width = tensor, width

    def block(self, c, x, a, h):
        rows = self.shape[2]
        if h is None:
            return (1, 1, rows, self.tensor * self.width), (c, x, 0, a)
        return (1, 1, rows, self.width), (c, x, 0, a * self.tensor + h)


def aligned(rows, width):
    return rows % 16 == 0 and width % 128 == 0


def cut(layout, value, c, x, a):
    shape, at = layout.block(c, x, a, None)
    start = [i * n for i, n in zip(at, shape)]
    return lax.dynamic_slice(value, start, shape).reshape(layout.shape[-2], layout.tensor * layout.width)


def call(kernel, name, grid, scalars, inputs, outputs, aliases):
    in_specs = [
        pl.BlockSpec(memory_space=pl.ANY) if block is None else pl.BlockSpec(block, at)
        for _, block, at in inputs
    ]
    grid_spec = pltpu.PrefetchScalarGridSpec(
        num_scalar_prefetch=1,
        grid=grid,
        in_specs=in_specs,
        out_specs=[pl.BlockSpec(block, at) for _, _, block, at in outputs],
    )
    return pl.pallas_call(
        kernel,
        grid_spec=grid_spec,
        out_shape=[jax.ShapeDtypeStruct(shape, dtype) for shape, dtype, _, _ in outputs],
        input_output_aliases=aliases,
        compiler_params=pltpu.CompilerParams(vmem_limit_bytes=vmem),
        cost_estimate=pl.CostEstimate(flops=20000000000, bytes_accessed=1000000, transcendentals=0),
        name=name,
    )(scalars, *[array for array, _, _ in inputs])


def pick_table(layout, value, here, half_shards):
    rows, wide = layout.shape[-2], 2 * layout.tensor * layout.width
    if not aligned(rows, layout.width):
        parts = [cut(layout, value, here[0], x, a) for a in range(half_shards) for x in range(2)]
        parts = [jnp.concatenate(parts[2 * a : 2 * a + 2], 1) for a in range(half_shards)]
        return jnp.stack(parts)

    def kernel(here, value_ref, out_ref):
        out_ref[0] = value_ref[...]

    return call(
        kernel,
        "pick",
        (half_shards,),
        here,
        [(value, (rows, wide), lambda a, here: (0, a * 2 + here[0]))],
        [((half_shards, rows, wide), value.dtype, (1, rows, wide), lambda a, here: (a, 0, 0))],
        {},
    )[0]


def add_split(layout, value, received, here, half_shards):
    rows, tensor, width = layout.shape[-2], layout.tensor, layout.width
    wide = tensor * width

    def got(x, a):
        return (a, 0, x) if layout.table else (x, 0, a)

    if not aligned(rows, width):
        halves = []
        for x in (1 - here[1], here[1]):
            parts = []
            for a in range(half_shards):
                first, _, last = got(x, a)
                part = lax.dynamic_slice(received, (first, 0, last * wide), (1, rows, wide))[0]
                parts.append(part + cut(layout, value, here[0], x, a))
            for y in (1 - here[2], here[2]):
                halves.append(lax.dynamic_slice_in_dim(jnp.stack(parts), y * width, width, 2))
        return halves

    def kernel(here, own_sent, own_kept, got_sent, got_kept, *out_refs):
        for y in range(tensor):

            @pl.when(here[2] == y)
            def _():
                for j, (own, got) in enumerate(((own_sent, got_sent), (own_kept, got_kept))):
                    lead = (0,) * (len(own.shape) - 2) + (slice(None),)
                    for h in range(2):
                        start = (y ^ h ^ 1) * width
                        columns = slice(start, start + width)
                        out_refs[2 * j + h][0] = own[lead + (columns,)] + got[0, :, columns]

    block = layout.block(0, 0, 0, None)[0]
    out = ((half_shards, rows, width), jnp.float32, (1, rows, width), lambda a, here: (a, 0, 0))
    return call(
        kernel,
        "add_split",
        (half_shards,),
        here,
        [
            (value, block, lambda a, here: layout.block(here[0], 1 - here[1], a, None)[1]),
            (value, block, lambda a, here: layout.block(here[0], here[1], a, None)[1]),
            (received, (1, rows, wide), lambda a, here: got(1 - here[1], a)),
            (received, (1, rows, wide), lambda a, here: got(here[1], a)),
        ],
        [out] * 4,
        {},
    )


def transposed_base(master, moment, here):
    width, model = master.shape[-2:]
    step = 256 if width % 256 == 0 else width
    if not aligned(model, width):
        start, shape = (here[0], here[1], here[2], 0, 0), (1, 1, 1, width, model)
        base = lax.dynamic_slice(master, start, shape) - (
            outer_rate * momentum_coef * momentum_coef
        ) * lax.dynamic_slice(moment, start, shape)
        return base[0, 0, 0].T

    def kernel(here, master_ref, moment_ref, out_ref):
        shape = (step, model)
        base = master_ref[...].reshape(shape) - (
            outer_rate * momentum_coef * momentum_coef
        ) * moment_ref[...].reshape(shape)
        out_ref[...] = base.T

    at = lambda i, here: (here[0], here[1], here[2], i, 0)
    block = (1, 1, 1, step, model)
    return call(
        kernel,
        "transposed_base",
        (width // step,),
        here,
        [(master, block, at), (moment, block, at)],
        [((model, width), jnp.float32, (model, step), lambda i, here: (0, i))],
        {},
    )[0]


def update(stacks, master, moment, here, before):
    width, model = master.shape[-2:]
    if not aligned(model, width):
        weights, velocity = before or (jnp.zeros_like(master), jnp.zeros_like(moment))
        for d in range(2 * len(stacks)):
            start = (here[0] ^ (d // 2), here[1] ^ (d % 2), here[2], 0, 0)
            shape = (1, 1, 1, width, model)
            mean = stacks[d // 2][d % 2].reshape(shape) * (1 / (4 * scale))
            new = momentum_coef * lax.dynamic_slice(moment, start, shape) + mean
            velocity = lax.dynamic_update_slice(velocity, new, start)
            new = lax.dynamic_slice(master, start, shape) - outer_rate * (mean + momentum_coef * new)
            weights = lax.dynamic_update_slice(weights, new, start)
        return weights, velocity
    count = len(stacks)

    def kernel(here, *refs):
        master_ref, moment_ref = refs[count : count + 2]
        weights_ref, velocity_ref = refs[-2:]

        def compute(summed_ref):
            mean = summed_ref[...].reshape(weights_ref.shape) * (1 / (4 * scale))
            velocity = momentum_coef * moment_ref[...] + mean
            velocity_ref[...] = velocity
            weights_ref[...] = master_ref[...] - outer_rate * (mean + momentum_coef * velocity)

        if count == 1:
            compute(refs[0])
        else:
            for j in range(count):
                pl.when(pl.program_id(0) // 2 == j)(lambda: compute(refs[j]))

    def stack_at(j):
        return lambda d, here: (jnp.clip(d - 2 * j, 0, 1), 0, 0)

    at = lambda d, here: (here[0] ^ (d // 2), here[1] ^ (d % 2), here[2], 0, 0)
    block = (1, 1, 1, width, model)
    out = (master.shape, jnp.float32, block, at)
    inputs = [(stack, (1, width, model), stack_at(j)) for j, stack in enumerate(stacks)]
    inputs += [(master, block, at), (moment, block, at)]
    aliases = {}
    if before is not None:
        inputs += [(value, None, None) for value in before]
        aliases = {count + 3: 0, count + 4: 1}
    return call(kernel, "update", (2 * count,), here, inputs, [out, out], aliases)


def place(layout, parts, here, half_shards):
    rows, width, tensor = layout.shape[-2], layout.width, layout.tensor
    if not aligned(rows, width):
        result = jnp.zeros(layout.shape, jnp.bfloat16)
        for j, part in enumerate(parts):
            for a in range(half_shards):
                at = here[0] ^ (j // 4), here[1] ^ (j // 2 % 2), a, here[2] ^ (j % 2)
                shape, at = layout.block(*at)
                start = [i * n for i, n in zip(at, shape)]
                result = lax.dynamic_update_slice(result, part[a].reshape(shape), start)
        return result

    def kernel(here, *refs):
        out_ref = refs[-1]
        for j in range(8):
            for y in range(tensor):

                @pl.when(here[2] == y)
                def _():
                    h = y ^ (j % 2)
                    c, x = here[0] ^ (j // 4), here[1] ^ (j // 2 % 2)
                    if layout.table:
                        for place in range(4):

                            @pl.when(c * 2 + x == place)
                            def _():
                                start = (place * tensor + h) * width
                                out_ref[:, start : start + width] = refs[j][0]

                    else:
                        out_ref[c, x, :, h * width : (h + 1) * width] = refs[j][0]

    if layout.table:
        block, out_at = (rows, 4 * tensor * width), lambda a, here: (0, a)
    else:
        block, out_at = (2, 2, rows, tensor * width), lambda a, here: (0, 0, 0, a)
    return call(
        kernel,
        "place",
        (half_shards,),
        here,
        [(part, (1, rows, width), lambda a, here: (a, 0, 0)) for part in parts],
        [(layout.shape, jnp.bfloat16, block, out_at)],
        {},
    )[0]


def local(expert_change, table_change, expert_master, expert_moment, table_master, table_moment):
    groups, shards, tensor = sizes = tuple(lax.axis_size(a) for a in axes)
    r, z, y = (lax.axis_index(a) for a in axes)
    core, x = r % 2, r // 2
    half_shards = shards // tensor
    here = jnp.stack([core, x, y]).astype(jnp.int32)
    other = jnp.stack([1 - core, x, y]).astype(jnp.int32)
    here_far = jnp.stack([core, x, 1 - y]).astype(jnp.int32)
    other_far = jnp.stack([1 - core, x, 1 - y]).astype(jnp.int32)

    def send(name, value, move):
        with jax.named_scope(name):
            return lax.ppermute(value, axes, pairs(sizes, move))

    def over_core(name, value):
        return send(name + "_core", value, lambda r, z, y: (r ^ 1, z, y))

    def over_x(name, value):
        return send(name + "_x", value, lambda r, z, y: (r ^ 2, z, y))

    def over_y(name, value):
        return send(name + "_y", value, lambda r, z, y: (r, z, y ^ 1))

    def over_z(name, value):
        with jax.named_scope(name + "_z"):
            return lax.all_to_all(value, "shard", split_axis=0, concat_axis=0, tiled=True)

    def index(value, i):
        return lax.dynamic_index_in_dim(value, i, 0, False)

    last = []

    def after(*values):
        if not last:
            return values if len(values) > 1 else values[0]
        values = lax.optimization_barrier((*values, last[0]))[:-1]
        return values if len(values) > 1 else values[0]

    def mark(value):
        last[:] = [value]
        return value

    def unmix(got):
        k = 1
        while k < shards:
            swap = (z & k) != 0
            got = [jnp.where(swap, got[i ^ k], got[i]) for i in range(shards)]
            k *= 2
        return got

    model = expert_master.shape[-1]
    mats, rows, expert_columns = expert_change.shape[1:]

    class Part:
        def __init__(self, name, layout, change, master, moment):
            self.name, self.layout, self.change = name, layout, change
            shape = (2, 2, tensor, layout.width, model)
            self.master, self.moment = master.reshape(shape), moment.reshape(shape)
            self.result = None

        def start(self):
            change = after(self.change)
            if self.layout.table:
                picked = pick_table(self.layout, change, other, half_shards)
            else:
                picked = index(change, 1 - core)
            self.got = over_core(self.name, mark(picked))

        def sum_core(self):
            change, got = after(self.change, self.got)
            sent = add_split(self.layout, change, got, here, half_shards)
            self.kept = sent[2:]
            far = mark((sent[0] * scale).astype(jnp.float16))
            self.received = [over_x(self.name + "_far", far)]
            self.sent_near = sent[1]

        def send_near(self):
            near = mark((after(self.sent_near) * scale).astype(jnp.float16))
            self.received.append(over_x(self.name + "_near", near))

        def bases(self):
            master, moment = after(self.master, self.moment)
            self.base = mark(transposed_base(master, moment, here))

        def sum_half(self, i):
            kept, received = after(self.kept[i], self.received[i])
            return mark((kept * scale + received.astype(jnp.float32)).astype(jnp.float16))

        def sum_far(self):
            self.far = over_y(self.name, self.sum_half(0))

        def sum_near(self):
            self.near = self.sum_half(1)

        def scatter(self):
            near, far = after(self.near, self.far)

            def of_shard(s):
                a = s % half_shards
                return jnp.where(s // half_shards == y, index(near, a), index(far, a))

            sent = [of_shard(z ^ k) for k in range(shards)]
            mark(sent[-1])
            self.sums = [sent[0]] + [
                send(f"{self.name}_z{k}", sent[k], lambda r, z, y: (r, z ^ k, y)) for k in range(1, shards)
            ]

        def low_part(self):
            received = after(self.received)
            base = self.base.reshape(received.shape)
            low = base - (outer_rate * (1 + momentum_coef) / (groups * scale)) * received.astype(jnp.float32)
            self.low = mark(low.astype(jnp.bfloat16))

        def copies_z(self):
            self.low = over_z(self.name + "_back", mark(after(self.low)))

        def gather(self):
            self.received = received = jnp.stack(unmix(after(*self.sums)))
            own = jnp.transpose(received, (2, 0, 1)).reshape(received.shape[2], model)
            own = mark(with_layout_constraint(own, Layout(major_to_minor=(0, 1))))
            self.near = over_x(self.name + "_gather", own)
            self.far = over_y(self.name + "_gather", own)
            self.own = own

        def gather_x(self):
            near = after(self.near)
            self.far2 = over_y(self.name + "_gather2", near)
            self.pair = mark(jnp.stack([self.own, near]).astype(jnp.float32))
            self.pair_core = over_core(self.name + "_gather", self.pair)

        def gather_y(self):
            far, far2 = after(self.far, self.far2)
            self.far_pair = mark(jnp.stack([far, far2]).astype(jnp.float32))
            self.far_core = over_core(self.name + "_gather2", self.far_pair)

        def wait(self, name):
            setattr(self, name, mark(after(getattr(self, name))))

        def update(self, *which):
            stacks = after(*[getattr(self, name) for name in which])
            stacks = stacks if len(which) > 1 else (stacks,)
            where = {"pair": here, "pair_core": other, "far_pair": here_far, "far_core": other_far}[which[0]]
            self.result = update(stacks, self.master, self.moment, where, self.result)
            mark(self.result[0])

        def copies_y(self):
            got = after(self.low)
            near = lax.dynamic_slice_in_dim(got, y * half_shards, half_shards, 0)
            far = mark(lax.dynamic_slice_in_dim(got, (1 - y) * half_shards, half_shards, 0))
            self.low_near = near
            self.low_far = over_y(self.name + "_back", far)
            self.low_near_x = over_x(self.name + "_back", near)

        def copies_x(self):
            far, near_x = after(self.low_far, self.low_near_x)
            mark(far)
            self.low_far_x = over_x(self.name + "_back2", far)
            self.parts = [self.low_near, far, near_x]
            self.parts_core = [over_core(self.name + "_back", part) for part in self.parts]

        def copies_core(self):
            far_x = mark(after(self.low_far_x))
            self.parts.append(far_x)
            self.parts_core.append(over_core(self.name + "_back2", far_x))

        def wait_core(self):
            self.parts_core = list(after(*self.parts_core))
            mark(self.parts_core[-1])

        def place(self):
            parts = after(*self.parts, *self.parts_core)
            self.copies = mark(place(self.layout, parts, here, half_shards))

    t = Part(
        "table",
        Table(rows, table_change.shape[2] // (4 * shards), half_shards, tensor),
        table_change[0],
        table_master,
        table_moment,
    )
    expert_layout = Expert(rows, expert_columns // shards, half_shards, tensor)
    e = Part(
        "expert", expert_layout, expert_change[0].reshape(expert_layout.shape), expert_master, expert_moment
    )
    e.start()
    t.start()
    e.sum_core()
    e.send_near()
    t.sum_core()
    e.sum_far()
    t.send_near()
    e.bases()
    e.sum_near()
    e.scatter()
    t.sum_far()
    t.bases()
    e.gather()
    t.sum_near()
    t.scatter()
    e.low_part()
    e.copies_z()
    e.wait("near")
    e.wait("far")
    e.gather_x()
    e.update("pair")
    e.wait("far2")
    e.gather_y()
    e.copies_y()
    t.gather()
    t.low_part()
    t.copies_z()
    e.update("pair_core")
    e.update("far_pair")
    e.update("far_core")
    t.wait("near")
    t.wait("far")
    e.wait("low_far")
    e.wait("low_near_x")
    t.wait("low")
    t.gather_x()
    e.copies_x()
    t.update("pair")
    t.update("pair_core")
    t.wait("far2")
    e.wait_core()
    e.wait("low_far_x")
    t.gather_y()
    e.copies_core()
    t.copies_y()
    t.update("far_pair")
    t.wait("low_near_x")
    t.wait("low_far")
    t.copies_x()
    t.update("far_core")
    e.place()
    t.wait_core()
    t.wait("low_far_x")
    t.copies_core()
    t.place()
    return (
        e.result[0].reshape(expert_master.shape),
        e.result[1].reshape(expert_master.shape),
        e.copies.reshape(mats, rows, expert_columns),
        t.result[0].reshape(table_master.shape),
        t.result[1].reshape(table_master.shape),
        t.copies,
    )


def solution(mesh):
    in_specs = (
        P("rep", None, "shard", "tp"),
        P("rep", "shard", "tp"),
        P(None, "shard", None),
        P(None, "shard", None),
        P("shard", None),
        P("shard", None),
    )
    out_specs = (
        P(None, "shard", None),
        P(None, "shard", None),
        P(None, "shard", "tp"),
        P("shard", None),
        P("shard", None),
        P("shard", "tp"),
    )
    return jax.shard_map(local, mesh=mesh, in_specs=in_specs, out_specs=out_specs, check_vma=False)
```

```python
import jax
import jax.numpy as jnp
from jax import lax
from jax.experimental import pallas as pl
from jax.experimental.layout import Layout, with_layout_constraint
from jax.experimental.pallas import tpu as pltpu
from jax.sharding import PartitionSpec as P

momentum_coef = 0.9
outer_rate = 0.7
axes = ("rep", "shard", "tp")
scale = 2048.0
vmem = 52 * 2**20


def pairs(mesh_sizes, move):
    groups, shards, tensor = mesh_sizes
    result = []
    for r in range(groups):
        for z in range(shards):
            for y in range(tensor):
                r2, z2, y2 = move(r, z, y)
                result.append(((r * shards + z) * tensor + y, (r2 * shards + z2) * tensor + y2))
    return result


class Table:
    table = True

    def __init__(self, rows, width, half_shards, tensor):
        self.shape = (rows, half_shards * 4 * tensor * width)
        self.tensor, self.width = tensor, width

    def block(self, c, x, a, h):
        rows = self.shape[0]
        if h is None:
            return (rows, self.tensor * self.width), (0, (a * 2 + c) * 2 + x)
        return (rows, self.width), (0, ((a * 2 + c) * 2 + x) * self.tensor + h)


class Expert:
    table = False

    def __init__(self, rows, width, half_shards, tensor):
        self.shape = (2, 2, rows, half_shards * tensor * width)
        self.tensor, self.width = tensor, width

    def block(self, c, x, a, h):
        rows = self.shape[2]
        if h is None:
            return (1, 1, rows, self.tensor * self.width), (c, x, 0, a)
        return (1, 1, rows, self.width), (c, x, 0, a * self.tensor + h)


def aligned(rows, width):
    return rows % 16 == 0 and width % 128 == 0


def cut(layout, value, c, x, a):
    shape, at = layout.block(c, x, a, None)
    start = [i * n for i, n in zip(at, shape)]
    return lax.dynamic_slice(value, start, shape).reshape(layout.shape[-2], layout.tensor * layout.width)


def call(kernel, name, grid, scalars, inputs, outputs, aliases):
    in_specs = [
        pl.BlockSpec(memory_space=pl.ANY) if block is None else pl.BlockSpec(block, at)
        for _, block, at in inputs
    ]
    grid_spec = pltpu.PrefetchScalarGridSpec(
        num_scalar_prefetch=1,
        grid=grid,
        in_specs=in_specs,
        out_specs=[pl.BlockSpec(block, at) for _, _, block, at in outputs],
    )
    return pl.pallas_call(
        kernel,
        grid_spec=grid_spec,
        out_shape=[jax.ShapeDtypeStruct(shape, dtype) for shape, dtype, _, _ in outputs],
        input_output_aliases=aliases,
        compiler_params=pltpu.CompilerParams(vmem_limit_bytes=vmem),
        cost_estimate=pl.CostEstimate(flops=20000000000, bytes_accessed=1000000, transcendentals=0),
        name=name,
    )(scalars, *[array for array, _, _ in inputs])


def pick_table(layout, value, here, half_shards):
    rows, wide = layout.shape[-2], 2 * layout.tensor * layout.width
    if not aligned(rows, layout.width):
        parts = [cut(layout, value, here[0], x, a) for a in range(half_shards) for x in range(2)]
        parts = [jnp.concatenate(parts[2 * a : 2 * a + 2], 1) for a in range(half_shards)]
        return jnp.stack(parts)

    def kernel(here, value_ref, out_ref):
        out_ref[0] = value_ref[...]

    return call(
        kernel,
        "pick",
        (half_shards,),
        here,
        [(value, (rows, wide), lambda a, here: (0, a * 2 + here[0]))],
        [((half_shards, rows, wide), value.dtype, (1, rows, wide), lambda a, here: (a, 0, 0))],
        {},
    )[0]


def add_split(layout, value, received, here, half_shards):
    rows, tensor, width = layout.shape[-2], layout.tensor, layout.width
    wide = tensor * width

    def got(x, a):
        return (a, 0, x) if layout.table else (x, 0, a)

    if not aligned(rows, width):
        halves = []
        for x in (1 - here[1], here[1]):
            parts = []
            for a in range(half_shards):
                first, _, last = got(x, a)
                part = lax.dynamic_slice(received, (first, 0, last * wide), (1, rows, wide))[0]
                parts.append(part + cut(layout, value, here[0], x, a))
            for y in (1 - here[2], here[2]):
                halves.append(lax.dynamic_slice_in_dim(jnp.stack(parts), y * width, width, 2))
        return halves

    def kernel(here, own_sent, own_kept, got_sent, got_kept, *out_refs):
        for y in range(tensor):

            @pl.when(here[2] == y)
            def _():
                for j, (own, got) in enumerate(((own_sent, got_sent), (own_kept, got_kept))):
                    lead = (0,) * (len(own.shape) - 2) + (slice(None),)
                    for h in range(2):
                        start = (y ^ h ^ 1) * width
                        columns = slice(start, start + width)
                        out_refs[2 * j + h][0] = own[lead + (columns,)] + got[0, :, columns]

    block = layout.block(0, 0, 0, None)[0]
    out = ((half_shards, rows, width), jnp.float32, (1, rows, width), lambda a, here: (a, 0, 0))
    return call(
        kernel,
        "add_split",
        (half_shards,),
        here,
        [
            (value, block, lambda a, here: layout.block(here[0], 1 - here[1], a, None)[1]),
            (value, block, lambda a, here: layout.block(here[0], here[1], a, None)[1]),
            (received, (1, rows, wide), lambda a, here: got(1 - here[1], a)),
            (received, (1, rows, wide), lambda a, here: got(here[1], a)),
        ],
        [out] * 4,
        {},
    )


def transposed_base(master, moment, here):
    width, model = master.shape[-2:]
    step = 256 if width % 256 == 0 else width
    if not aligned(model, width):
        start, shape = (here[0], here[1], here[2], 0, 0), (1, 1, 1, width, model)
        base = lax.dynamic_slice(master, start, shape) - (
            outer_rate * momentum_coef * momentum_coef
        ) * lax.dynamic_slice(moment, start, shape)
        return base[0, 0, 0].T

    def kernel(here, master_ref, moment_ref, out_ref):
        shape = (step, model)
        base = master_ref[...].reshape(shape) - (
            outer_rate * momentum_coef * momentum_coef
        ) * moment_ref[...].reshape(shape)
        out_ref[...] = base.T

    at = lambda i, here: (here[0], here[1], here[2], i, 0)
    block = (1, 1, 1, step, model)
    return call(
        kernel,
        "transposed_base",
        (width // step,),
        here,
        [(master, block, at), (moment, block, at)],
        [((model, width), jnp.float32, (model, step), lambda i, here: (0, i))],
        {},
    )[0]


def update(stacks, master, moment, here, before):
    width, model = master.shape[-2:]
    if not aligned(model, width):
        weights, velocity = before or (jnp.zeros_like(master), jnp.zeros_like(moment))
        for d in range(2 * len(stacks)):
            start = (here[0] ^ (d // 2), here[1] ^ (d % 2), here[2], 0, 0)
            shape = (1, 1, 1, width, model)
            mean = stacks[d // 2][d % 2].reshape(shape) * (1 / (4 * scale))
            new = momentum_coef * lax.dynamic_slice(moment, start, shape) + mean
            velocity = lax.dynamic_update_slice(velocity, new, start)
            new = lax.dynamic_slice(master, start, shape) - outer_rate * (mean + momentum_coef * new)
            weights = lax.dynamic_update_slice(weights, new, start)
        return weights, velocity
    count = len(stacks)

    def kernel(here, *refs):
        master_ref, moment_ref = refs[count : count + 2]
        weights_ref, velocity_ref = refs[-2:]

        def compute(summed_ref):
            mean = summed_ref[...].reshape(weights_ref.shape) * (1 / (4 * scale))
            velocity = momentum_coef * moment_ref[...] + mean
            velocity_ref[...] = velocity
            weights_ref[...] = master_ref[...] - outer_rate * (mean + momentum_coef * velocity)

        if count == 1:
            compute(refs[0])
        else:
            for j in range(count):
                pl.when(pl.program_id(0) // 2 == j)(lambda: compute(refs[j]))

    def stack_at(j):
        return lambda d, here: (jnp.clip(d - 2 * j, 0, 1), 0, 0)

    at = lambda d, here: (here[0] ^ (d // 2), here[1] ^ (d % 2), here[2], 0, 0)
    block = (1, 1, 1, width, model)
    out = (master.shape, jnp.float32, block, at)
    inputs = [(stack, (1, width, model), stack_at(j)) for j, stack in enumerate(stacks)]
    inputs += [(master, block, at), (moment, block, at)]
    aliases = {}
    if before is not None:
        inputs += [(value, None, None) for value in before]
        aliases = {count + 3: 0, count + 4: 1}
    return call(kernel, "update", (2 * count,), here, inputs, [out, out], aliases)


def place(layout, parts, here, half_shards):
    rows, width, tensor = layout.shape[-2], layout.width, layout.tensor
    if not aligned(rows, width):
        result = jnp.zeros(layout.shape, jnp.bfloat16)
        for j, part in enumerate(parts):
            for a in range(half_shards):
                at = here[0] ^ (j // 4), here[1] ^ (j // 2 % 2), a, here[2] ^ (j % 2)
                shape, at = layout.block(*at)
                start = [i * n for i, n in zip(at, shape)]
                result = lax.dynamic_update_slice(result, part[a].reshape(shape), start)
        return result

    def kernel(here, *refs):
        out_ref = refs[-1]
        for j in range(8):
            for y in range(tensor):

                @pl.when(here[2] == y)
                def _():
                    h = y ^ (j % 2)
                    c, x = here[0] ^ (j // 4), here[1] ^ (j // 2 % 2)
                    if layout.table:
                        for place in range(4):

                            @pl.when(c * 2 + x == place)
                            def _():
                                start = (place * tensor + h) * width
                                out_ref[:, start : start + width] = refs[j][0]

                    else:
                        out_ref[c, x, :, h * width : (h + 1) * width] = refs[j][0]

    if layout.table:
        block, out_at = (rows, 4 * tensor * width), lambda a, here: (0, a)
    else:
        block, out_at = (2, 2, rows, tensor * width), lambda a, here: (0, 0, 0, a)
    return call(
        kernel,
        "place",
        (half_shards,),
        here,
        [(part, (1, rows, width), lambda a, here: (a, 0, 0)) for part in parts],
        [(layout.shape, jnp.bfloat16, block, out_at)],
        {},
    )[0]


def local(expert_change, table_change, expert_master, expert_moment, table_master, table_moment):
    groups, shards, tensor = sizes = tuple(lax.axis_size(a) for a in axes)
    r, z, y = (lax.axis_index(a) for a in axes)
    core, x = r % 2, r // 2
    half_shards = shards // tensor
    here = jnp.stack([core, x, y]).astype(jnp.int32)
    other = jnp.stack([1 - core, x, y]).astype(jnp.int32)
    here_far = jnp.stack([core, x, 1 - y]).astype(jnp.int32)
    other_far = jnp.stack([1 - core, x, 1 - y]).astype(jnp.int32)

    def send(name, value, move):
        with jax.named_scope(name):
            return lax.ppermute(value, axes, pairs(sizes, move))

    def over_core(name, value):
        return send(name + "_core", value, lambda r, z, y: (r ^ 1, z, y))

    def over_x(name, value):
        return send(name + "_x", value, lambda r, z, y: (r ^ 2, z, y))

    def over_y(name, value):
        return send(name + "_y", value, lambda r, z, y: (r, z, y ^ 1))

    def over_z(name, value):
        with jax.named_scope(name + "_z"):
            return lax.all_to_all(value, "shard", split_axis=0, concat_axis=0, tiled=True)

    def index(value, i):
        return lax.dynamic_index_in_dim(value, i, 0, False)

    last = []

    def after(*values):
        if not last:
            return values if len(values) > 1 else values[0]
        values = lax.optimization_barrier((*values, last[0]))[:-1]
        return values if len(values) > 1 else values[0]

    def mark(value):
        last[:] = [value]
        return value

    def unmix(got):
        k = 1
        while k < shards:
            swap = (z & k) != 0
            got = [jnp.where(swap, got[i ^ k], got[i]) for i in range(shards)]
            k *= 2
        return got

    model = expert_master.shape[-1]
    mats, rows, expert_columns = expert_change.shape[1:]

    class Part:
        def __init__(self, name, layout, change, master, moment):
            self.name, self.layout, self.change = name, layout, change
            shape = (2, 2, tensor, layout.width, model)
            self.master, self.moment = master.reshape(shape), moment.reshape(shape)
            self.result = None

        def start(self):
            change = after(self.change)
            if self.layout.table:
                picked = pick_table(self.layout, change, other, half_shards)
            else:
                picked = index(change, 1 - core)
            self.got = over_core(self.name, mark(picked))

        def sum_core(self):
            change, got = after(self.change, self.got)
            sent = add_split(self.layout, change, got, here, half_shards)
            self.kept = sent[2:]
            far = mark((sent[0] * scale).astype(jnp.float16))
            self.received = [over_x(self.name + "_far", far)]
            self.sent_near = sent[1]

        def send_near(self):
            near = mark((after(self.sent_near) * scale).astype(jnp.float16))
            self.received.append(over_x(self.name + "_near", near))

        def bases(self):
            master, moment = after(self.master, self.moment)
            self.base = mark(transposed_base(master, moment, here))

        def sum_half(self, i):
            kept, received = after(self.kept[i], self.received[i])
            return mark((kept * scale + received.astype(jnp.float32)).astype(jnp.float16))

        def sum_far(self):
            self.far = over_y(self.name, self.sum_half(0))

        def sum_near(self):
            self.near = self.sum_half(1)

        def scatter(self):
            near, far = after(self.near, self.far)

            def of_shard(s):
                a = s % half_shards
                return jnp.where(s // half_shards == y, index(near, a), index(far, a))

            sent = [of_shard(z ^ k) for k in range(shards)]
            mark(sent[-1])
            self.sums = [sent[0]] + [
                send(f"{self.name}_z{k}", sent[k], lambda r, z, y: (r, z ^ k, y)) for k in range(1, shards)
            ]

        def low_part(self):
            received = after(self.received)
            base = self.base.reshape(received.shape)
            low = base - (outer_rate * (1 + momentum_coef) / (groups * scale)) * received.astype(jnp.float32)
            self.low = mark(low.astype(jnp.bfloat16))

        def copies_z(self):
            self.low = over_z(self.name + "_back", mark(after(self.low)))

        def gather(self):
            self.received = received = jnp.stack(unmix(after(*self.sums)))
            own = jnp.transpose(received, (2, 0, 1)).reshape(received.shape[2], model)
            own = mark(with_layout_constraint(own, Layout(major_to_minor=(0, 1))))
            self.near = over_x(self.name + "_gather", own)
            self.far = over_y(self.name + "_gather", own)
            self.own = own

        def gather_x(self):
            near = after(self.near)
            self.far2 = over_y(self.name + "_gather2", near)
            self.pair = mark(jnp.stack([self.own, near]).astype(jnp.float32))
            self.pair_core = over_core(self.name + "_gather", self.pair)

        def gather_y(self):
            far, far2 = after(self.far, self.far2)
            self.far_pair = mark(jnp.stack([far, far2]).astype(jnp.float32))
            self.far_core = over_core(self.name + "_gather2", self.far_pair)

        def wait(self, name):
            setattr(self, name, mark(after(getattr(self, name))))

        def update(self, *which):
            stacks = after(*[getattr(self, name) for name in which])
            stacks = stacks if len(which) > 1 else (stacks,)
            where = {"pair": here, "pair_core": other, "far_pair": here_far, "far_core": other_far}[which[0]]
            self.result = update(stacks, self.master, self.moment, where, self.result)
            mark(self.result[0])

        def copies_y(self):
            got = after(self.low)
            near = lax.dynamic_slice_in_dim(got, y * half_shards, half_shards, 0)
            far = mark(lax.dynamic_slice_in_dim(got, (1 - y) * half_shards, half_shards, 0))
            self.low_near = near
            self.low_far = over_y(self.name + "_back", far)
            self.low_near_x = over_x(self.name + "_back", near)

        def copies_x(self):
            far, near_x = after(self.low_far, self.low_near_x)
            mark(far)
            self.low_far_x = over_x(self.name + "_back2", far)
            self.parts = [self.low_near, far, near_x]
            self.parts_core = [over_core(self.name + "_back", part) for part in self.parts]

        def copies_core(self):
            far_x = mark(after(self.low_far_x))
            self.parts.append(far_x)
            self.parts_core.append(over_core(self.name + "_back2", far_x))

        def wait_core(self):
            self.parts_core = list(after(*self.parts_core))
            mark(self.parts_core[-1])

        def place(self):
            parts = after(*self.parts, *self.parts_core)
            self.copies = mark(place(self.layout, parts, here, half_shards))

    t = Part(
        "table",
        Table(rows, table_change.shape[2] // (4 * shards), half_shards, tensor),
        table_change[0],
        table_master,
        table_moment,
    )
    expert_layout = Expert(rows, expert_columns // shards, half_shards, tensor)
    e = Part(
        "expert", expert_layout, expert_change[0].reshape(expert_layout.shape), expert_master, expert_moment
    )
    e.start()
    t.start()
    e.sum_core()
    e.send_near()
    t.sum_core()
    e.sum_far()
    t.send_near()
    e.bases()
    e.sum_near()
    e.scatter()
    t.sum_far()
    t.bases()
    e.gather()
    t.sum_near()
    t.scatter()
    e.low_part()
    e.copies_z()
    e.wait("near")
    e.wait("far")
    e.gather_x()
    e.update("pair")
    e.wait("far2")
    e.gather_y()
    t.gather()
    e.copies_y()
    t.low_part()
    t.copies_z()
    e.update("pair_core")
    e.update("far_pair")
    e.update("far_core")
    t.wait("near")
    t.wait("far")
    e.wait("low_far")
    e.wait("low_near_x")
    t.wait("low")
    t.gather_x()
    e.copies_x()
    t.update("pair")
    t.update("pair_core")
    t.wait("far2")
    e.wait_core()
    e.wait("low_far_x")
    t.gather_y()
    e.copies_core()
    t.copies_y()
    t.update("far_pair")
    t.wait("low_near_x")
    t.wait("low_far")
    t.copies_x()
    t.update("far_core")
    e.place()
    t.wait_core()
    t.wait("low_far_x")
    t.copies_core()
    t.place()
    return (
        e.result[0].reshape(expert_master.shape),
        e.result[1].reshape(expert_master.shape),
        e.copies.reshape(mats, rows, expert_columns),
        t.result[0].reshape(table_master.shape),
        t.result[1].reshape(table_master.shape),
        t.copies,
    )


def solution(mesh):
    in_specs = (
        P("rep", None, "shard", "tp"),
        P("rep", "shard", "tp"),
        P(None, "shard", None),
        P(None, "shard", None),
        P("shard", None),
        P("shard", None),
    )
    out_specs = (
        P(None, "shard", None),
        P(None, "shard", None),
        P(None, "shard", "tp"),
        P("shard", None),
        P("shard", None),
        P("shard", "tp"),
    )
    return jax.shard_map(local, mesh=mesh, in_specs=in_specs, out_specs=out_specs, check_vma=False)
```

```python
import jax
import jax.numpy as jnp
from jax import lax
from jax.experimental import pallas as pl
from jax.experimental.layout import Layout, with_layout_constraint
from jax.experimental.pallas import tpu as pltpu
from jax.sharding import PartitionSpec as P

momentum_coef = 0.9
outer_rate = 0.7
axes = ("rep", "shard", "tp")
scale = 2048.0
vmem = 52 * 2**20


def pairs(mesh_sizes, move):
    groups, shards, tensor = mesh_sizes
    result = []
    for r in range(groups):
        for z in range(shards):
            for y in range(tensor):
                r2, z2, y2 = move(r, z, y)
                result.append(((r * shards + z) * tensor + y, (r2 * shards + z2) * tensor + y2))
    return result


class Table:
    table = True

    def __init__(self, rows, width, half_shards, tensor):
        self.shape = (rows, half_shards * 4 * tensor * width)
        self.tensor, self.width = tensor, width

    def block(self, c, x, a, h):
        rows = self.shape[0]
        if h is None:
            return (rows, self.tensor * self.width), (0, (a * 2 + c) * 2 + x)
        return (rows, self.width), (0, ((a * 2 + c) * 2 + x) * self.tensor + h)


class Expert:
    table = False

    def __init__(self, rows, width, half_shards, tensor):
        self.shape = (2, 2, rows, half_shards * tensor * width)
        self.tensor, self.width = tensor, width

    def block(self, c, x, a, h):
        rows = self.shape[2]
        if h is None:
            return (1, 1, rows, self.tensor * self.width), (c, x, 0, a)
        return (1, 1, rows, self.width), (c, x, 0, a * self.tensor + h)


def aligned(rows, width):
    return rows % 16 == 0 and width % 128 == 0


def cut(layout, value, c, x, a):
    shape, at = layout.block(c, x, a, None)
    start = [i * n for i, n in zip(at, shape)]
    return lax.dynamic_slice(value, start, shape).reshape(layout.shape[-2], layout.tensor * layout.width)


def call(kernel, name, grid, scalars, inputs, outputs, aliases):
    in_specs = [
        pl.BlockSpec(memory_space=pl.ANY) if block is None else pl.BlockSpec(block, at)
        for _, block, at in inputs
    ]
    grid_spec = pltpu.PrefetchScalarGridSpec(
        num_scalar_prefetch=1,
        grid=grid,
        in_specs=in_specs,
        out_specs=[pl.BlockSpec(block, at) for _, _, block, at in outputs],
    )
    return pl.pallas_call(
        kernel,
        grid_spec=grid_spec,
        out_shape=[jax.ShapeDtypeStruct(shape, dtype) for shape, dtype, _, _ in outputs],
        input_output_aliases=aliases,
        compiler_params=pltpu.CompilerParams(vmem_limit_bytes=vmem),
        cost_estimate=pl.CostEstimate(flops=20000000000, bytes_accessed=1000000, transcendentals=0),
        name=name,
    )(scalars, *[array for array, _, _ in inputs])


def pick_table(layout, value, here, half_shards):
    rows, wide = layout.shape[-2], 2 * layout.tensor * layout.width
    if not aligned(rows, layout.width):
        parts = [cut(layout, value, here[0], x, a) for a in range(half_shards) for x in range(2)]
        parts = [jnp.concatenate(parts[2 * a : 2 * a + 2], 1) for a in range(half_shards)]
        return jnp.stack(parts)

    def kernel(here, value_ref, out_ref):
        out_ref[0] = value_ref[...]

    return call(
        kernel,
        "pick",
        (half_shards,),
        here,
        [(value, (rows, wide), lambda a, here: (0, a * 2 + here[0]))],
        [((half_shards, rows, wide), value.dtype, (1, rows, wide), lambda a, here: (a, 0, 0))],
        {},
    )[0]


def add_split(layout, value, received, here, half_shards):
    rows, tensor, width = layout.shape[-2], layout.tensor, layout.width
    wide = tensor * width

    def got(x, a):
        return (a, 0, x) if layout.table else (x, 0, a)

    if not aligned(rows, width):
        halves = []
        for x in (1 - here[1], here[1]):
            parts = []
            for a in range(half_shards):
                first, _, last = got(x, a)
                part = lax.dynamic_slice(received, (first, 0, last * wide), (1, rows, wide))[0]
                parts.append(part + cut(layout, value, here[0], x, a))
            for y in (1 - here[2], here[2]):
                halves.append(lax.dynamic_slice_in_dim(jnp.stack(parts), y * width, width, 2))
        return halves

    def kernel(here, own_sent, own_kept, got_sent, got_kept, *out_refs):
        for y in range(tensor):

            @pl.when(here[2] == y)
            def _():
                for j, (own, got) in enumerate(((own_sent, got_sent), (own_kept, got_kept))):
                    lead = (0,) * (len(own.shape) - 2) + (slice(None),)
                    for h in range(2):
                        start = (y ^ h ^ 1) * width
                        columns = slice(start, start + width)
                        out_refs[2 * j + h][0] = own[lead + (columns,)] + got[0, :, columns]

    block = layout.block(0, 0, 0, None)[0]
    out = ((half_shards, rows, width), jnp.float32, (1, rows, width), lambda a, here: (a, 0, 0))
    return call(
        kernel,
        "add_split",
        (half_shards,),
        here,
        [
            (value, block, lambda a, here: layout.block(here[0], 1 - here[1], a, None)[1]),
            (value, block, lambda a, here: layout.block(here[0], here[1], a, None)[1]),
            (received, (1, rows, wide), lambda a, here: got(1 - here[1], a)),
            (received, (1, rows, wide), lambda a, here: got(here[1], a)),
        ],
        [out] * 4,
        {},
    )


def transposed_base(master, moment, here):
    width, model = master.shape[-2:]
    step = 256 if width % 256 == 0 else width
    if not aligned(model, width):
        start, shape = (here[0], here[1], here[2], 0, 0), (1, 1, 1, width, model)
        base = lax.dynamic_slice(master, start, shape) - (
            outer_rate * momentum_coef * momentum_coef
        ) * lax.dynamic_slice(moment, start, shape)
        return base[0, 0, 0].T

    def kernel(here, master_ref, moment_ref, out_ref):
        shape = (step, model)
        base = master_ref[...].reshape(shape) - (
            outer_rate * momentum_coef * momentum_coef
        ) * moment_ref[...].reshape(shape)
        out_ref[...] = base.T

    at = lambda i, here: (here[0], here[1], here[2], i, 0)
    block = (1, 1, 1, step, model)
    return call(
        kernel,
        "transposed_base",
        (width // step,),
        here,
        [(master, block, at), (moment, block, at)],
        [((model, width), jnp.float32, (model, step), lambda i, here: (0, i))],
        {},
    )[0]


def update(stacks, master, moment, here, before):
    width, model = master.shape[-2:]
    if not aligned(model, width):
        weights, velocity = before or (jnp.zeros_like(master), jnp.zeros_like(moment))
        for d in range(2 * len(stacks)):
            start = (here[0] ^ (d // 2), here[1] ^ (d % 2), here[2], 0, 0)
            shape = (1, 1, 1, width, model)
            mean = stacks[d // 2][d % 2].reshape(shape) * (1 / (4 * scale))
            new = momentum_coef * lax.dynamic_slice(moment, start, shape) + mean
            velocity = lax.dynamic_update_slice(velocity, new, start)
            new = lax.dynamic_slice(master, start, shape) - outer_rate * (mean + momentum_coef * new)
            weights = lax.dynamic_update_slice(weights, new, start)
        return weights, velocity
    count = len(stacks)

    def kernel(here, *refs):
        master_ref, moment_ref = refs[count : count + 2]
        weights_ref, velocity_ref = refs[-2:]

        def compute(summed_ref):
            mean = summed_ref[...].reshape(weights_ref.shape) * (1 / (4 * scale))
            velocity = momentum_coef * moment_ref[...] + mean
            velocity_ref[...] = velocity
            weights_ref[...] = master_ref[...] - outer_rate * (mean + momentum_coef * velocity)

        if count == 1:
            compute(refs[0])
        else:
            for j in range(count):
                pl.when(pl.program_id(0) // 2 == j)(lambda: compute(refs[j]))

    def stack_at(j):
        return lambda d, here: (jnp.clip(d - 2 * j, 0, 1), 0, 0)

    at = lambda d, here: (here[0] ^ (d // 2), here[1] ^ (d % 2), here[2], 0, 0)
    block = (1, 1, 1, width, model)
    out = (master.shape, jnp.float32, block, at)
    inputs = [(stack, (1, width, model), stack_at(j)) for j, stack in enumerate(stacks)]
    inputs += [(master, block, at), (moment, block, at)]
    aliases = {}
    if before is not None:
        inputs += [(value, None, None) for value in before]
        aliases = {count + 3: 0, count + 4: 1}
    return call(kernel, "update", (2 * count,), here, inputs, [out, out], aliases)


def place(layout, parts, here, half_shards):
    rows, width, tensor = layout.shape[-2], layout.width, layout.tensor
    if not aligned(rows, width):
        result = jnp.zeros(layout.shape, jnp.bfloat16)
        for j, part in enumerate(parts):
            for a in range(half_shards):
                at = here[0] ^ (j // 4), here[1] ^ (j // 2 % 2), a, here[2] ^ (j % 2)
                shape, at = layout.block(*at)
                start = [i * n for i, n in zip(at, shape)]
                result = lax.dynamic_update_slice(result, part[a].reshape(shape), start)
        return result

    def kernel(here, *refs):
        out_ref = refs[-1]
        for j in range(8):
            for y in range(tensor):

                @pl.when(here[2] == y)
                def _():
                    h = y ^ (j % 2)
                    c, x = here[0] ^ (j // 4), here[1] ^ (j // 2 % 2)
                    if layout.table:
                        for place in range(4):

                            @pl.when(c * 2 + x == place)
                            def _():
                                start = (place * tensor + h) * width
                                out_ref[:, start : start + width] = refs[j][0]

                    else:
                        out_ref[c, x, :, h * width : (h + 1) * width] = refs[j][0]

    if layout.table:
        block, out_at = (rows, 4 * tensor * width), lambda a, here: (0, a)
    else:
        block, out_at = (2, 2, rows, tensor * width), lambda a, here: (0, 0, 0, a)
    return call(
        kernel,
        "place",
        (half_shards,),
        here,
        [(part, (1, rows, width), lambda a, here: (a, 0, 0)) for part in parts],
        [(layout.shape, jnp.bfloat16, block, out_at)],
        {},
    )[0]


def local(expert_change, table_change, expert_master, expert_moment, table_master, table_moment):
    groups, shards, tensor = sizes = tuple(lax.axis_size(a) for a in axes)
    r, z, y = (lax.axis_index(a) for a in axes)
    core, x = r % 2, r // 2
    half_shards = shards // tensor
    here = jnp.stack([core, x, y]).astype(jnp.int32)
    other = jnp.stack([1 - core, x, y]).astype(jnp.int32)
    here_far = jnp.stack([core, x, 1 - y]).astype(jnp.int32)
    other_far = jnp.stack([1 - core, x, 1 - y]).astype(jnp.int32)

    def send(name, value, move):
        with jax.named_scope(name):
            return lax.ppermute(value, axes, pairs(sizes, move))

    def over_core(name, value):
        return send(name + "_core", value, lambda r, z, y: (r ^ 1, z, y))

    def over_x(name, value):
        return send(name + "_x", value, lambda r, z, y: (r ^ 2, z, y))

    def over_y(name, value):
        return send(name + "_y", value, lambda r, z, y: (r, z, y ^ 1))

    def over_z(name, value):
        with jax.named_scope(name + "_z"):
            return lax.all_to_all(value, "shard", split_axis=0, concat_axis=0, tiled=True)

    def index(value, i):
        return lax.dynamic_index_in_dim(value, i, 0, False)

    last = []

    def after(*values):
        if not last:
            return values if len(values) > 1 else values[0]
        values = lax.optimization_barrier((*values, last[0]))[:-1]
        return values if len(values) > 1 else values[0]

    def mark(value):
        last[:] = [value]
        return value

    def unmix(got):
        k = 1
        while k < shards:
            swap = (z & k) != 0
            got = [jnp.where(swap, got[i ^ k], got[i]) for i in range(shards)]
            k *= 2
        return got

    model = expert_master.shape[-1]
    mats, rows, expert_columns = expert_change.shape[1:]

    class Part:
        def __init__(self, name, layout, change, master, moment):
            self.name, self.layout, self.change = name, layout, change
            shape = (2, 2, tensor, layout.width, model)
            self.master, self.moment = master.reshape(shape), moment.reshape(shape)
            self.result = None

        def start(self):
            change = after(self.change)
            if self.layout.table:
                picked = pick_table(self.layout, change, other, half_shards)
            else:
                picked = index(change, 1 - core)
            self.got = over_core(self.name, mark(picked))

        def sum_core(self):
            change, got = after(self.change, self.got)
            sent = add_split(self.layout, change, got, here, half_shards)
            self.kept = sent[2:]
            far = mark((sent[0] * scale).astype(jnp.float16))
            self.received = [over_x(self.name + "_far", far)]
            self.sent_near = sent[1]

        def send_near(self):
            near = mark((after(self.sent_near) * scale).astype(jnp.float16))
            self.received.append(over_x(self.name + "_near", near))

        def bases(self):
            master, moment = after(self.master, self.moment)
            self.base = mark(transposed_base(master, moment, here))

        def sum_half(self, i):
            kept, received = after(self.kept[i], self.received[i])
            return mark((kept * scale + received.astype(jnp.float32)).astype(jnp.float16))

        def sum_far(self):
            self.far = over_y(self.name, self.sum_half(0))

        def sum_near(self):
            self.near = self.sum_half(1)

        def scatter(self):
            near, far = after(self.near, self.far)

            def of_shard(s):
                a = s % half_shards
                return jnp.where(s // half_shards == y, index(near, a), index(far, a))

            sent = [of_shard(z ^ k) for k in range(shards)]
            mark(sent[-1])
            self.sums = [sent[0]] + [
                send(f"{self.name}_z{k}", sent[k], lambda r, z, y: (r, z ^ k, y)) for k in range(1, shards)
            ]

        def low_part(self):
            received = after(self.received)
            base = self.base.reshape(received.shape)
            low = base - (outer_rate * (1 + momentum_coef) / (groups * scale)) * received.astype(jnp.float32)
            self.low = mark(low.astype(jnp.bfloat16))

        def copies_z(self):
            self.low = over_z(self.name + "_back", mark(after(self.low)))

        def gather(self):
            self.received = received = jnp.stack(unmix(after(*self.sums)))
            own = jnp.transpose(received, (2, 0, 1)).reshape(received.shape[2], model)
            own = mark(with_layout_constraint(own, Layout(major_to_minor=(0, 1))))
            self.near = over_x(self.name + "_gather", own)
            self.far = over_y(self.name + "_gather", own)
            self.own = own

        def gather_x(self):
            near = after(self.near)
            self.far2 = over_y(self.name + "_gather2", near)
            self.pair = mark(jnp.stack([self.own, near]).astype(jnp.float32))
            self.pair_core = over_core(self.name + "_gather", self.pair)

        def gather_y(self):
            far, far2 = after(self.far, self.far2)
            self.far_pair = mark(jnp.stack([far, far2]).astype(jnp.float32))
            self.far_core = over_core(self.name + "_gather2", self.far_pair)

        def wait(self, name):
            setattr(self, name, mark(after(getattr(self, name))))

        def update(self, *which):
            stacks = after(*[getattr(self, name) for name in which])
            stacks = stacks if len(which) > 1 else (stacks,)
            where = {"pair": here, "pair_core": other, "far_pair": here_far, "far_core": other_far}[which[0]]
            self.result = update(stacks, self.master, self.moment, where, self.result)
            mark(self.result[0])

        def copies_y(self):
            got = after(self.low)
            near = lax.dynamic_slice_in_dim(got, y * half_shards, half_shards, 0)
            far = mark(lax.dynamic_slice_in_dim(got, (1 - y) * half_shards, half_shards, 0))
            self.low_near = near
            self.low_far = over_y(self.name + "_back", far)
            self.low_near_x = over_x(self.name + "_back", near)

        def copies_x(self):
            far, near_x = after(self.low_far, self.low_near_x)
            mark(far)
            self.low_far_x = over_x(self.name + "_back2", far)
            self.parts = [self.low_near, far, near_x]
            self.parts_core = [over_core(self.name + "_back", part) for part in self.parts]

        def copies_core(self):
            far_x = mark(after(self.low_far_x))
            self.parts.append(far_x)
            self.parts_core.append(over_core(self.name + "_back2", far_x))

        def wait_core(self):
            self.parts_core = list(after(*self.parts_core))
            mark(self.parts_core[-1])

        def place(self):
            parts = after(*self.parts, *self.parts_core)
            self.copies = mark(place(self.layout, parts, here, half_shards))

    t = Part(
        "table",
        Table(rows, table_change.shape[2] // (4 * shards), half_shards, tensor),
        table_change[0],
        table_master,
        table_moment,
    )
    expert_layout = Expert(rows, expert_columns // shards, half_shards, tensor)
    e = Part(
        "expert", expert_layout, expert_change[0].reshape(expert_layout.shape), expert_master, expert_moment
    )
    e.start()
    t.start()
    e.sum_core()
    e.send_near()
    t.sum_core()
    e.sum_far()
    t.send_near()
    e.bases()
    e.sum_near()
    e.scatter()
    t.sum_far()
    t.bases()
    e.gather()
    t.sum_near()
    t.scatter()
    e.low_part()
    e.copies_z()
    e.wait("near")
    e.wait("far")
    e.gather_x()
    e.update("pair")
    e.wait("far2")
    e.gather_y()
    t.gather()
    t.low_part()
    e.copies_y()
    t.copies_z()
    e.update("pair_core")
    e.update("far_pair")
    e.update("far_core")
    t.wait("near")
    t.wait("far")
    e.wait("low_far")
    e.wait("low_near_x")
    t.wait("low")
    t.gather_x()
    e.copies_x()
    t.update("pair")
    t.update("pair_core")
    t.wait("far2")
    e.wait_core()
    e.wait("low_far_x")
    t.copies_y()
    t.gather_y()
    e.copies_core()
    t.update("far_pair")
    t.wait("low_near_x")
    t.wait("low_far")
    t.copies_x()
    t.update("far_core")
    e.place()
    t.wait_core()
    t.wait("low_far_x")
    t.copies_core()
    t.place()
    return (
        e.result[0].reshape(expert_master.shape),
        e.result[1].reshape(expert_master.shape),
        e.copies.reshape(mats, rows, expert_columns),
        t.result[0].reshape(table_master.shape),
        t.result[1].reshape(table_master.shape),
        t.copies,
    )


def solution(mesh):
    in_specs = (
        P("rep", None, "shard", "tp"),
        P("rep", "shard", "tp"),
        P(None, "shard", None),
        P(None, "shard", None),
        P("shard", None),
        P("shard", None),
    )
    out_specs = (
        P(None, "shard", None),
        P(None, "shard", None),
        P(None, "shard", "tp"),
        P("shard", None),
        P("shard", None),
        P("shard", "tp"),
    )
    return jax.shard_map(local, mesh=mesh, in_specs=in_specs, out_specs=out_specs, check_vma=False)
```
